256 devices in a mesh: row: 4 (over y), col: 8 (over z), feat: 8 (over x, core).
Axes of the slice: x: 4, y: 4, z: 8, core: 2. Of those that a mesh axis runs over, the one named last changes fastest.
Arguments:
- features: bfloat16 [16384, 128], P(('col', 'row'), 'feat'), may hold values from -6 to 6
- weight_in: bfloat16 [128, 256], P(None, 'feat'), may hold values from -0.5 to 0.5
- bias: float32 [256], P('feat'), may hold values from -3 to 3
- weight_out: bfloat16 [256, 172], P('feat'), may hold values from -50 to 50
- adj_tiles: bfloat16 [4, 8, 384, 128, 128], P('row', 'col'), may hold values from 0 to 0.039794922
- tile_rows: int32 [4, 8, 384], P('row', 'col'), may hold values from 0 to 31, as said below
- tile_cols: int32 [4, 8, 384], P('row', 'col'), may hold values from 0 to 15, as said below
- tile_live: int32 [4, 8], P('row', 'col'), may hold values from 48 to 384, as said below
- labels: int32 [16384], P(('row', 'col')), may hold values from 0 to 171
- label_mask: int32 [16384], P(('row', 'col')), may hold values from 0 to 1, as said below
Outputs:
- loss: float32 [], replicated
- grad_w1: float32 [128, 256], P(None, 'feat')
- grad_b1: float32 [256], P('feat')
- grad_w2: float32 [256, 172], P('feat')
The draws below stay inside these ranges and needn't reach their ends.
Inputs may be any that keep to these rules, and one draw needn't show every extreme that they name: `tile_rows`: the slots of one row-column block name distinct tiles. `tile_cols`: the slots of one row-column block name distinct tiles. `tile_live`: some row-column block uses all 384 slots. `label_mask`: at least one node is labelled.
All inputs are finite; a program needn't handle non-finite values.
Results may differ from the reference program's by a relative error of at most 0.0075.
Values may be sent and summed in bfloat16 or wider, within the bound.
No kernel may reach another device: no remote copies, remote signals or barrier semaphores. Data moves between devices by JAX's collectives and lax.ppermute only.
A program may use at most 64 MiB of HBM per device.

```python
import math
import jax
import jax.numpy as jnp
from jax import lax

FIN = 128
HID = 256
CLASSES = 172
TILE = 128
NODE_DEV = 512
TMAX = 384
NODES = 16384
N_ROW = 4
N_COL = 8


def tile_places(key):
    row_blocks = NODE_DEV * N_COL // TILE
    col_blocks = NODE_DEV * N_ROW // TILE
    device_keys = jax.random.split(key, N_ROW * N_COL)
    orders = jax.vmap(lambda single: jax.random.permutation(single, row_blocks * col_blocks))(device_keys)
    return (orders[:, :TMAX].reshape(N_ROW, N_COL, TMAX).astype(jnp.int32), col_blocks)


def draw_tile_rows(key, part):
    places, col_blocks = tile_places(jax.random.fold_in(key, 7))
    return (places // col_blocks).astype(jnp.int32)


def draw_tile_cols(key, part):
    places, col_blocks = tile_places(jax.random.fold_in(key, 7))
    return (places % col_blocks).astype(jnp.int32)


def draw_tile_live(key, part):
    key = jax.random.fold_in(key, 3)
    first_key, second_key = jax.random.split(key)
    lowest = max(1, TMAX // 8)
    counts = jax.random.randint(first_key, (N_ROW * N_COL,), lowest, max(lowest + 1, TMAX // 2 + 1), dtype=jnp.int32)
    chosen = jax.random.randint(second_key, (), 0, N_ROW * N_COL, dtype=jnp.int32)
    counts = jnp.where(jnp.arange(N_ROW * N_COL, dtype=jnp.int32) == chosen, TMAX, counts)
    return counts.reshape(N_ROW, N_COL).astype(jnp.int32)


def draw_label_mask(key, part):
    key = jax.random.fold_in(key, 5)
    position = jnp.arange(NODES, dtype=jnp.int32)
    share = 150 + 450 * position // NODES
    ticket = jax.random.randint(key, (NODES,), 0, 1000, dtype=jnp.int32)
    marked = (ticket < share).astype(jnp.int32)
    return marked.at[0].set(1)


def draw_weight_out(key, part):
    key = jax.random.fold_in(key, 9)
    key_list = jax.random.split(key, 1)
    scale = 2.5 / math.sqrt(HID)
    base = jnp.clip(jax.random.normal(key_list[0], (HID, CLASSES), jnp.float32), -4.0, 4.0) * scale
    return base.astype(jnp.bfloat16)


def place_ends(drawn, own_key, smallest, high):
    dims = drawn.shape
    spot = [jax.random.randint(jax.random.fold_in(own_key, axis), (), 0, dims[axis]) for axis in range(len(dims))]
    drawn = drawn.at[tuple(spot)].set(smallest)
    longest = dims.index(max(dims))
    spot[longest] = (spot[longest] + 1) % dims[longest]
    return drawn.at[tuple(spot)].set(high)


def steps_of(key, dims, shards, low, high):
    def one(axis_at, shards_of):
        heights = jax.random.uniform(jax.random.fold_in(jax.random.fold_in(key, 6), axis_at), (shards_of,), jnp.float32, low / len(shards), high / len(shards))
        return jnp.repeat(jnp.exp(heights), dims[axis_at] // shards_of).reshape((-1,) + (1,) * (len(dims) - axis_at - 1))

    factor_of = one(*shards[0])
    for cut in shards[1:]:
        factor_of = factor_of * one(*cut)
    return factor_of


def normal_values(key, shape, deviation, bound, cuts=(), kind=jnp.bfloat16):
    drawn = deviation * jax.random.normal(key, shape, jnp.float32)
    if cuts:
        drawn = drawn * steps_of(key, shape, cuts, -0.22, 0.18)
    return jnp.clip(drawn, -bound, bound).astype(kind)


def setup_inputs(seed: int = 0) -> dict:
    seeds = jax.random.split(jax.random.key(seed), 11)
    return {
        "features": normal_values(seeds[0], (NODES, FIN), 1.0, 6.0, ((0, 32), (1, 8))),
        "weight_in": normal_values(seeds[1], (FIN, HID), FIN ** -0.5, 0.5, ((1, 8),)),
        "bias": normal_values(seeds[2], (HID,), 0.5, 3.0, ((0, 8),), jnp.float32),
        "weight_out": draw_weight_out(jax.random.fold_in(seeds[10], 71), 0),
        "adj_tiles": jnp.clip(0.039794922 * jax.random.uniform(seeds[4], (N_ROW, N_COL, TMAX, TILE, TILE), jnp.float32) ** steps_of(seeds[4], (N_ROW, N_COL, TMAX, TILE, TILE), ((0, 4), (1, 8)), -0.2, 0.2), 0.0, 0.039794922).astype(jnp.bfloat16),
        "tile_rows": draw_tile_rows(jax.random.fold_in(seeds[10], 71), 0),
        "tile_cols": draw_tile_cols(jax.random.fold_in(seeds[10], 71), 0),
        "tile_live": draw_tile_live(jax.random.fold_in(seeds[10], 71), 0),
        "labels": place_ends(jax.random.randint(seeds[8], (NODES,), 0, CLASSES), jax.random.fold_in(seeds[8], 1), 0, CLASSES - 1).astype(jnp.int32),
        "label_mask": draw_label_mask(jax.random.fold_in(seeds[10], 71), 0),
    }


def gelu_tanh(values):
    return jax.nn.gelu(values, approximate=True)

def tile_sums(node_blocks, adj_tiles, tile_rows, tile_cols, tile_live, transpose):
    row_blocks = NODE_DEV * N_COL // TILE
    col_blocks = NODE_DEV * N_ROW // TILE
    groups = N_ROW * N_COL
    width = node_blocks.shape[2]
    tiles_all = adj_tiles.reshape(groups, TMAX, TILE, TILE)
    rows_all = tile_rows.reshape(groups, TMAX).astype(jnp.int32)
    cols_all = tile_cols.reshape(groups, TMAX).astype(jnp.int32)
    live_all = tile_live.reshape(groups).astype(jnp.int32)
    group_ids = jnp.arange(groups, dtype=jnp.int32)

    def advance(carry, item):
        slot_tiles, slot_rows, slot_cols, slot_live, group = item
        row_index = group // N_COL * row_blocks + slot_rows
        col_index = group % N_COL * col_blocks + slot_cols
        slot_weight = (jnp.arange(TMAX, dtype=jnp.int32) < slot_live).astype(jnp.float32)
        weighted = slot_tiles.astype(jnp.float32) * slot_weight[:, None, None]
        if transpose:
            source = node_blocks[row_index].astype(jnp.float32)
            terms = jnp.einsum('tij,tih->tjh', weighted, source)
            carry = carry.at[col_index].add(terms)
        else:
            source = node_blocks[col_index].astype(jnp.float32)
            terms = jnp.einsum('tij,tjh->tih', weighted, source)
            carry = carry.at[row_index].add(terms)
        return (carry, None)
    initial = jnp.zeros((node_blocks.shape[0], TILE, width), jnp.float32)
    result, unused = lax.scan(advance, initial, (tiles_all, rows_all, cols_all, live_all, group_ids))
    return result.reshape(node_blocks.shape[0] * TILE, width)

def reference(features, weight_in, bias, weight_out, adj_tiles, tile_rows, tile_cols, tile_live, labels, label_mask):
    projected = jnp.dot(features, weight_in, preferred_element_type=jnp.float32).astype(jnp.bfloat16)
    gathered = tile_sums(projected.reshape(-1, TILE, HID), adj_tiles, tile_rows, tile_cols, tile_live, False)
    preact = gathered + bias.astype(jnp.float32)
    hidden = gelu_tanh(preact).astype(jnp.bfloat16)
    logits = jnp.dot(hidden, weight_out, preferred_element_type=jnp.float32)
    count = jnp.sum(label_mask).astype(jnp.float32)
    weights = label_mask.astype(jnp.float32) / count
    shifted = logits - lax.optimization_barrier(jnp.max(logits, axis=1, keepdims=True))
    expsum = lax.optimization_barrier(jnp.sum(jnp.exp(shifted), axis=1, keepdims=True))
    onehot = (labels[:, None] == jnp.arange(CLASSES, dtype=jnp.int32)[None, :]).astype(jnp.float32)
    row_loss = jnp.log(expsum[:, 0]) - lax.optimization_barrier(jnp.sum(shifted * onehot, axis=1))
    loss = jnp.sum(row_loss * weights)
    grad_logits = ((jnp.exp(shifted) / expsum - onehot) * weights[:, None]).astype(jnp.bfloat16)
    grad_w2 = jnp.dot(hidden.T, grad_logits, preferred_element_type=jnp.float32)
    grad_hidden = jnp.dot(grad_logits, weight_out.T, preferred_element_type=jnp.float32)
    grad_preact = jax.vjp(gelu_tanh, preact)[1](grad_hidden)[0].astype(jnp.bfloat16)
    grad_b1 = lax.optimization_barrier(jnp.sum(grad_preact.astype(jnp.float32), axis=0))
    grad_proj = tile_sums(grad_preact.reshape(-1, TILE, HID), adj_tiles, tile_rows, tile_cols, tile_live, True).astype(jnp.bfloat16)
    grad_w1 = jnp.dot(features.T, grad_proj, preferred_element_type=jnp.float32)
    return (loss, grad_w1, grad_b1, grad_w2)
```

```python
import functools

import jax
import jax.numpy as jnp
from jax import lax
from jax.experimental import pallas as pl
from jax.experimental.pallas import tpu as pltpu
from jax.sharding import PartitionSpec as P

CLASSES = 172
TILE = 128
REST = CLASSES - TILE
SLOTS = 24
GELU_SCALE = 0.7978845608028654
GELU_CUBE = 0.044715
F32 = jnp.float32
BF16 = jnp.bfloat16


def dot(a, b, contract=((1,), (0,))):
    return lax.dot_general(a, b, (contract, ((), ())), preferred_element_type=F32)


def gelu_parts(v):
    squared = v * v
    t = jnp.tanh(GELU_SCALE * v * (1.0 + GELU_CUBE * squared))
    return squared, t


def aggregate_kernel(rows_ref, cols_ref, live_ref, x_ref, tiles_ref, out_ref, acc_ref):
    step = pl.program_id(0)
    live = live_ref[0]

    @pl.when(step == 0)
    def _():
        acc_ref[...] = jnp.zeros_like(acc_ref)

    @pl.when(step * SLOTS < live)
    def _():
        for k in range(SLOTS):
            slot = step * SLOTS + k
            col = cols_ref[slot]
            row = rows_ref[slot]
            start = pl.multiple_of((col % 4) * TILE, TILE)
            block = x_ref[col // 4, :, pl.ds(start, TILE)]
            block = jnp.where(slot < live, block, jnp.zeros_like(block))
            acc_ref[row] += dot(block, tiles_ref[k], ((1,), (1,)))

    @pl.when(step == pl.num_programs(0) - 1)
    def _():
        out_ref[...] = acc_ref[...].astype(BF16)


def aggregate(x_all, tiles, rows, cols, live, row_blocks):
    slots = tiles.shape[0]
    feats = x_all.shape[1]

    def tile_map(step, rows, cols, live):
        return (jnp.minimum(step, (live[0] - 1) // SLOTS), 0, 0)

    return pl.pallas_call(
        aggregate_kernel,
        out_shape=jax.ShapeDtypeStruct((row_blocks, feats, TILE), BF16),
        grid_spec=pltpu.PrefetchScalarGridSpec(
            num_scalar_prefetch=3,
            grid=(slots // SLOTS,),
            in_specs=[
                pl.BlockSpec(x_all.shape, lambda *_: (0, 0, 0)),
                pl.BlockSpec((SLOTS, TILE, TILE), tile_map),
            ],
            out_specs=pl.BlockSpec((row_blocks, feats, TILE), lambda *_: (0, 0, 0)),
            scratch_shapes=[pltpu.VMEM((row_blocks, feats, TILE), F32)],
        ),
    )(rows, cols, live, x_all, tiles)


def pack_kernel(parts_ref, weights_ref, out_ref):
    total = jnp.sum(parts_ref[...].astype(F32), axis=0).astype(BF16)
    nodes = total.shape[0]
    for k in range(out_ref.shape[0]):
        out_ref[k, :nodes, :] = total
        out_ref[k, nodes:, :] = weights_ref[...]


def node_kernel(all_ref, own_ref, labels_ref, mask_ref, out_ref, y_ref):
    groups = all_ref.shape[0]
    blocks = 4
    for f in range(groups):
        for b in range(blocks):
            y_ref[16 * f : 16 * f + 16, TILE * b : TILE * b + TILE] = all_ref[f, 16 * b : 16 * b + 16, :]
    y = y_ref[...]
    base = 16 * blocks
    w1 = all_ref[:, base : base + 32, :].reshape(32 * groups, TILE)
    w2a = all_ref[:, base + 32 : base + 64, :].reshape(32 * groups, TILE)
    w2b = all_ref[:, base + 64 : base + 96, :].reshape(32 * groups, TILE)

    def bias_of(block):
        wide = block.astype(F32)
        return wide[:, REST : REST + 1] + wide[:, REST + 1 : REST + 2] + wide[:, REST + 2 : REST + 3]

    preact = dot(w1, y) + bias_of(w2b)
    _, t = gelu_parts(preact)
    hidden = (0.5 * preact * (1.0 + t)).astype(BF16)
    logits_a = dot(w2a, hidden, ((0,), (0,)))
    logits_b = dot(w2b, hidden, ((0,), (0,)))[:48]
    labels = labels_ref[...]
    mask = mask_ref[...].astype(F32)
    class_a = lax.broadcasted_iota(jnp.int32, logits_a.shape, 0)
    class_b = lax.broadcasted_iota(jnp.int32, logits_b.shape, 0) + TILE
    logits_b = jnp.where(class_b < CLASSES, logits_b, -jnp.inf)
    top = jnp.maximum(
        jnp.max(logits_a, axis=0, keepdims=True), jnp.max(logits_b, axis=0, keepdims=True)
    )
    shifted_a = logits_a - top
    shifted_b = logits_b - top
    exp_a = jnp.exp(shifted_a)
    exp_b = jnp.exp(shifted_b)
    expsum = jnp.sum(exp_a, axis=0, keepdims=True) + jnp.sum(exp_b, axis=0, keepdims=True)
    hit_a = class_a == labels
    hit_b = class_b == labels
    picked = jnp.sum(jnp.where(hit_a, shifted_a, 0.0), axis=0, keepdims=True) + jnp.sum(
        jnp.where(hit_b, shifted_b, 0.0), axis=0, keepdims=True
    )
    loss = jnp.sum((jnp.log(expsum) - picked) * mask)
    count = jnp.sum(mask)
    inverse = 1.0 / expsum
    grad_a = ((exp_a * inverse - hit_a.astype(F32)) * mask).astype(BF16)
    grad_b = ((exp_b * inverse - hit_b.astype(F32)) * mask).astype(BF16)

    own_w1 = own_ref[:32, :]
    own_w2a = own_ref[32:64, :]
    own_w2b = own_ref[64:96, :]
    own_pre = dot(own_w1, y) + bias_of(own_w2b)
    squared, own_t = gelu_parts(own_pre)
    own_hidden = (0.5 * own_pre * (1.0 + own_t)).astype(BF16)
    slope = 0.5 * (1.0 + own_t) + 0.5 * own_pre * (1.0 - own_t * own_t) * (
        GELU_SCALE * (1.0 + 3.0 * GELU_CUBE * squared)
    )
    grad_hidden = dot(own_w2a, grad_a) + dot(own_w2b[:, :48], grad_b)
    grad_pre = (grad_hidden * slope).astype(BF16)
    grad_b1 = jnp.sum(grad_pre.astype(F32), axis=1, keepdims=True)
    grad_w1 = dot(grad_pre, y, ((1,), (1,)))
    grad_w2a = dot(own_hidden, grad_a, ((1,), (1,)))
    grad_w2b = dot(own_hidden, grad_b, ((1,), (1,)))
    lane = lax.broadcasted_iota(jnp.int32, (32, TILE), 1)
    sub = lax.broadcasted_iota(jnp.int32, (32, TILE), 0)
    wide = jnp.concatenate([grad_w2b, jnp.zeros((32, TILE - 48), F32)], axis=1)
    extra = jnp.where(sub == 0, loss, jnp.where(sub == 1, count, 0.0))
    last = jnp.where(
        lane < REST, wide, jnp.where(lane == REST, grad_b1, jnp.where(lane == REST + 1, extra, 0.0))
    )
    for k in range(out_ref.shape[0]):
        out_ref[k, :32, :] = grad_w1
        out_ref[k, 32:64, :] = grad_w2a
        out_ref[k, 64:, :] = last


def middle_kernel(parts_ref, out_ref):
    total = jnp.sum(parts_ref[...], axis=0)
    upper = total.astype(BF16).astype(F32)
    rest = total - upper
    shape = (32, TILE)
    lane = lax.broadcasted_iota(jnp.int32, shape, 1)
    moved = pltpu.roll(rest[64:], 2, 1)
    tail = jnp.where((lane >= REST + 2) & (lane < REST + 4), moved, upper[64:])
    for k in range(out_ref.shape[0]):
        out_ref[k, :64, :] = upper[:64].astype(BF16)
        out_ref[k, 64:, :] = tail.astype(BF16)


def final_kernel(parts_ref, w1_ref, w2_ref, b1_ref, loss_ref):
    total = jnp.sum(parts_ref[...].astype(F32), axis=0)
    tail = total[64:]
    tail = tail + pltpu.roll(tail, TILE - 2, 1)
    count = tail[1:2, REST + 1 : REST + 2]
    inverse = 1.0 / count
    w1_ref[...] = total[:32] * inverse
    w2_ref[:, :TILE] = total[32:64] * inverse
    w2_ref[:, TILE:] = total[64:, :REST] * inverse
    b1_ref[...] = tail[:, REST : REST + 1] * inverse
    loss_ref[...] = tail[0:1, REST + 1 : REST + 2] * inverse


def call(kernel, out_shape, *args, scratch=()):
    return pl.pallas_call(kernel, out_shape=out_shape, scratch_shapes=scratch)(*args)


def on_device(
    features,
    weight_in,
    bias,
    weight_out,
    adj_tiles,
    tile_rows,
    tile_cols,
    tile_live,
    labels,
    label_mask,
):
    n_row, n_col, n_feat = lax.axis_size("row"), lax.axis_size("col"), lax.axis_size("feat")
    row_blocks = features.shape[0] * n_col // TILE

    x_mine = features.T
    x_all = lax.all_to_all(jnp.broadcast_to(x_mine, (n_row, *x_mine.shape)), "row", 0, 0)
    partial = aggregate(
        x_all,
        adj_tiles.reshape(adj_tiles.shape[2:]),
        tile_rows.reshape(-1),
        tile_cols.reshape(-1),
        tile_live.reshape(-1),
        row_blocks,
    )
    feats = x_mine.shape[0]
    parts = lax.all_to_all(partial.reshape(n_col, -1, TILE), "col", 0, 0)

    def rounded(v):
        return lax.reduce_precision(v, 8, 7)

    high = rounded(bias)
    middle = rounded(bias - high)
    low = rounded(bias - high - middle)
    bias_lanes = jnp.stack([high, middle, low], axis=1).astype(BF16)
    tail = jnp.concatenate(
        [weight_out[:, TILE:], bias_lanes, jnp.zeros((32, TILE - REST - 3), BF16)], axis=1
    )
    own = jnp.concatenate([weight_in.T, weight_out[:, :TILE], tail], axis=0)
    message_rows = parts.shape[1] + own.shape[0]
    message = call(pack_kernel, jax.ShapeDtypeStruct((n_feat, message_rows, TILE), BF16), parts, own)
    gathered = lax.all_to_all(message, "feat", 0, 0)
    grads = call(
        node_kernel,
        jax.ShapeDtypeStruct((n_row, 96, TILE), F32),
        gathered,
        own,
        labels.reshape(1, -1),
        label_mask.reshape(1, -1),
        scratch=[pltpu.VMEM((feats * n_feat, features.shape[0]), BF16)],
    )
    grads = lax.all_to_all(grads, "row", 0, 0)
    grads = call(middle_kernel, jax.ShapeDtypeStruct((n_col, 96, TILE), BF16), grads)
    grads = lax.all_to_all(grads, "col", 0, 0)
    w1, w2, b1, loss = call(
        final_kernel,
        (
            jax.ShapeDtypeStruct((32, TILE), F32),
            jax.ShapeDtypeStruct((32, CLASSES), F32),
            jax.ShapeDtypeStruct((32, 1), F32),
            jax.ShapeDtypeStruct((1, 1), F32),
        ),
        grads,
    )
    return (loss.reshape(()), w1.T, b1.reshape(-1), w2)


def solution(mesh):
    in_specs = (
        P(("col", "row"), "feat"),
        P(None, "feat"),
        P("feat"),
        P("feat", None),
        P("row", "col", None, None, None),
        P("row", "col", None),
        P("row", "col", None),
        P("row", "col"),
        P(("row", "col")),
        P(("row", "col")),
    )
    out_specs = (P(), P(None, "feat"), P("feat"), P("feat", None))
    return jax.shard_map(
        on_device, mesh=mesh, in_specs=in_specs, out_specs=out_specs, check_vma=False
    )
```

```python
import functools

import jax
import jax.numpy as jnp
from jax import lax
from jax.experimental import pallas as pl
from jax.experimental.pallas import tpu as pltpu
from jax.sharding import PartitionSpec as P

CLASSES = 172
TILE = 128
REST = CLASSES - TILE
HALF = TILE // 2
GELU_SCALE = 0.7978845608028654
GELU_CUBE = 0.044715
COST = 60000000
F32 = jnp.float32
BF16 = jnp.bfloat16
IN_VMEM = pl.BlockSpec(memory_space=pltpu.VMEM)
IN_SMEM = pl.BlockSpec(memory_space=pltpu.SMEM)

def dot(a, b, contract=((1,), (0,))):
    return lax.dot_general(a, b, (contract, ((), ())), preferred_element_type=F32)

def gelu_parts(v):
    squared = v * v
    t = jnp.tanh(GELU_SCALE * v * (1.0 + GELU_CUBE * squared))
    return squared, t

def call(kernel, out_shape, *args, scalars=0, scratch=(), limit=16 * 2**20, cost=None):
    placed = args[:scalars] + tuple(
        pltpu.with_memory_space_constraint(arg, pltpu.VMEM) for arg in args[scalars:]
    )
    many = isinstance(out_shape, tuple)
    return pl.pallas_call(
        kernel,
        out_shape=out_shape,
        in_specs=[IN_SMEM] * scalars + [IN_VMEM] * (len(args) - scalars),
        out_specs=(IN_VMEM,) * len(out_shape) if many else IN_VMEM,
        scratch_shapes=scratch,
        compiler_params=pltpu.CompilerParams(vmem_limit_bytes=limit),
        cost_estimate=cost,
    )(*placed)

def pair_kernel(x_ref, other_ref, out_ref):
    first = lax.axis_index("core") == 0
    mine, other = x_ref[...], other_ref[...]
    feats = mine.shape[0]
    out_ref[:feats, :] = jnp.where(first, mine, other)
    out_ref[feats:, :] = jnp.where(first, other, mine)


def load_kernel(tiles_ref, out_ref, sems):
    chunk = tiles_ref.shape[0] // sems.shape[0]
    copies = []
    for k in range(sems.shape[0]):
        part = pl.ds(k * chunk, chunk)
        copies.append(pltpu.make_async_copy(tiles_ref.at[part], out_ref.at[part], sems.at[k]))
    for copy in copies:
        copy.start()
    for copy in copies:
        copy.wait()


def setup_kernel(live_ref, rows_ref, cols_ref, w1_ref, w2_ref, bias_ref, slots_ref, weights_ref):
    inverse(live_ref, rows_ref, cols_ref, slots_ref)
    pack_weights(w1_ref, w2_ref, bias_ref, weights_ref)


def inverse(live_ref, rows_ref, cols_ref, out_ref):
    places = out_ref.shape[1]
    slots = rows_ref.shape[2]
    slot = lax.broadcasted_iota(jnp.int32, (1, slots), 1)
    rows = rows_ref[0]
    place = ((rows >> 2) * 2 + (rows & 1)) * (places // 16) + cols_ref[0]
    mine = (slot < live_ref[0, 0]) & (((rows >> 1) & 1) == lax.axis_index("core"))
    place = jnp.where(mine, place, -1)
    here = lax.broadcasted_iota(jnp.int32, (places, slots), 0) == place
    onehot = jnp.where(here, 1.0, 0.0).astype(BF16)
    number = lax.broadcasted_iota(jnp.int32, (8, slots), 1) + 1
    digit = lax.broadcasted_iota(jnp.int32, (8, slots), 0)
    digits = jnp.where(digit == 0, number & 127, jnp.where(digit == 1, number >> 7, 0))
    found = dot(digits.astype(F32).astype(BF16), onehot, ((1,), (1,)))
    out_ref[...] = (found[0:1] + 128.0 * found[1:2]).astype(jnp.int32) - 1


def aggregate_kernel(slot_ref, x0_ref, x1_ref, x2_ref, x3_ref, tiles_ref, out_ref, all_ref):
    feats, nodes = x0_ref.shape
    row, n_row = lax.axis_index("row"), lax.axis_size("row")
    for k, part in enumerate((x0_ref, x1_ref, x2_ref, x3_ref)):
        source = lax.rem(row + n_row - k, n_row)
        all_ref[:, pl.ds(pl.multiple_of(source * nodes, TILE), nodes)] = part[...]
    x_all = all_ref[...]
    groups = out_ref.shape[0]
    col_blocks = slot_ref.shape[1] // (2 * groups)
    for group in range(groups):
        strips = []
        for block in (2 * group, 2 * group + 1):
            tiles = []
            for j in range(col_blocks):
                slot = slot_ref[0, block * col_blocks + j]
                tile = tiles_ref[jnp.maximum(slot, 0)]
                tiles.append(jnp.where(slot >= 0, tile, jnp.zeros_like(tile)))
            strips.append(jnp.concatenate(tiles, 1))
        wide = dot(x_all, jnp.concatenate(strips, 0), ((1,), (1,))).astype(BF16)
        out_ref[group, :feats, :] = wide[:, :TILE]
        out_ref[group, feats:, :] = wide[:, TILE:]


def pack_weights(w1_ref, w2_ref, bias_ref, out_ref):
    shape = (32, TILE)
    lane = lax.broadcasted_iota(jnp.int32, shape, 1)
    sub = lax.broadcasted_iota(jnp.int32, shape, 0)
    row = jnp.concatenate([bias_ref[...], jnp.zeros((1, TILE - 32), F32)], axis=1)
    bias = jnp.sum(jnp.where(lane == sub, row, 0.0), axis=1, keepdims=True)
    high = bias.astype(BF16).astype(F32)
    middle = (bias - high).astype(BF16).astype(F32)
    low = bias - high - middle
    rest = jnp.concatenate(
        [w2_ref[:, TILE:].astype(F32), jnp.zeros((32, TILE - REST), F32)], axis=1
    )
    for place, part in ((REST, high), (REST + 1, middle), (REST + 2, low)):
        rest = jnp.where(lane == place, part, rest)
    out_ref[:32, :] = w1_ref[...]
    out_ref[32:64, :] = w2_ref[:, :TILE]
    out_ref[64:, :] = rest.astype(BF16)

def total_kernel(parts_ref, weights_ref, out_ref):
    total = jnp.sum(parts_ref[...].astype(F32), axis=0).astype(BF16)
    rows = total.shape[0]
    for k in range(out_ref.shape[0]):
        out_ref[k, :rows, :] = total
        out_ref[k, rows:, :] = weights_ref[...]

def lanes16():
    return lax.broadcasted_iota(jnp.int32, (16, TILE), 1)

def is_fine(lane):
    return (lane == REST) | (lane == REST + 1) | (lane == HALF + REST)

def split_tail(tail):
    upper = tail.astype(BF16).astype(F32)
    moved = pltpu.roll(tail - upper, 2, 1)
    return jnp.where(is_fine(lanes16() - 2), moved, upper).astype(BF16)

def join_tail(tail):
    return jnp.where(is_fine(lanes16()), tail + pltpu.roll(tail, TILE - 2, 1), tail)

def node_kernel(all_ref, own_ref, labels_ref, mask_ref, out_ref, y_ref):
    groups = all_ref.shape[0]
    for f in range(groups):
        for b in range(2):
            feat, node = 32 * (f // 2), TILE * (2 * (f % 2) + b)
            y_ref[feat : feat + 32, node : node + TILE] = all_ref[f, 32 * b : 32 * b + 32, :]
    y = y_ref[...]
    w1 = all_ref[:, 64:96, :].reshape(32 * groups, TILE)
    w2a = all_ref[:, 96:128, :].reshape(32 * groups, TILE)
    w2b = all_ref[:, 128:, :].reshape(32 * groups, TILE)

    def bias_of(block):
        wide = block.astype(F32)
        return wide[:, REST : REST + 1] + wide[:, REST + 1 : REST + 2] + wide[:, REST + 2 : REST + 3]

    preact = dot(w1, y) + bias_of(w2b)
    _, t = gelu_parts(preact)
    hidden = (0.5 * preact * (1.0 + t)).astype(BF16)
    logits_a = dot(w2a, hidden, ((0,), (0,)))
    logits_b = dot(w2b, hidden, ((0,), (0,)))[:48]
    labels = labels_ref[...]
    mask = mask_ref[...].astype(F32)
    class_a = lax.broadcasted_iota(jnp.int32, logits_a.shape, 0)
    class_b = lax.broadcasted_iota(jnp.int32, logits_b.shape, 0) + TILE
    logits_b = jnp.where(class_b < CLASSES, logits_b, -jnp.inf)
    top = jnp.maximum(
        jnp.max(logits_a, axis=0, keepdims=True), jnp.max(logits_b, axis=0, keepdims=True)
    )
    shifted_a = logits_a - top
    shifted_b = logits_b - top
    exp_a = jnp.exp(shifted_a)
    exp_b = jnp.exp(shifted_b)
    expsum = jnp.sum(exp_a, axis=0, keepdims=True) + jnp.sum(exp_b, axis=0, keepdims=True)
    hit_a = class_a == labels
    hit_b = class_b == labels
    picked = jnp.sum(jnp.where(hit_a, shifted_a, 0.0), axis=0, keepdims=True) + jnp.sum(
        jnp.where(hit_b, shifted_b, 0.0), axis=0, keepdims=True
    )
    loss = jnp.sum((jnp.log(expsum) - picked) * mask)
    count = jnp.sum(mask)
    inverse = 1.0 / expsum
    grad_a = ((exp_a * inverse - hit_a.astype(F32)) * mask).astype(BF16)
    grad_b = ((exp_b * inverse - hit_b.astype(F32)) * mask).astype(BF16)

    own_w1 = own_ref[:32, :]
    own_w2a = own_ref[32:64, :]
    own_w2b = own_ref[64:, :]
    own_pre = dot(own_w1, y) + bias_of(own_w2b)
    squared, own_t = gelu_parts(own_pre)
    own_hidden = (0.5 * own_pre * (1.0 + own_t)).astype(BF16)
    slope = 0.5 * (1.0 + own_t) + 0.5 * own_pre * (1.0 - own_t * own_t) * (
        GELU_SCALE * (1.0 + 3.0 * GELU_CUBE * squared)
    )
    grad_hidden = dot(own_w2a, grad_a) + dot(own_w2b[:, :48], grad_b)
    grad_pre = (grad_hidden * slope).astype(BF16)
    grad_b1 = jnp.sum(grad_pre.astype(F32), axis=1, keepdims=True)
    grad_w1 = dot(grad_pre, y, ((1,), (1,))).astype(BF16)
    grad_w2a = dot(own_hidden, grad_a, ((1,), (1,))).astype(BF16)
    grad_w2b = dot(own_hidden, grad_b, ((1,), (1,)))
    lane = lanes16()
    sub = lax.broadcasted_iota(jnp.int32, lane.shape, 0)
    wide = jnp.concatenate([grad_w2b, jnp.zeros((32, TILE - 48), F32)], axis=1)
    extra = jnp.where(sub == 0, loss, jnp.where(sub == 1, count, 0.0))
    tail = jnp.where(lane < HALF, wide[:16], pltpu.roll(wide[16:], HALF, 1))
    tail = jnp.where(lane == REST, grad_b1[:16], tail)
    tail = jnp.where(lane == REST + 1, extra, tail)
    tail = jnp.where(lane == HALF + REST, grad_b1[16:], tail)
    tail = split_tail(tail)
    for k in range(out_ref.shape[0]):
        out_ref[k, :32, :] = grad_w1
        out_ref[k, 32:64, :] = grad_w2a
        out_ref[k, 64:, :] = tail

def middle_kernel(parts_ref, out_ref):
    total = jnp.sum(parts_ref[...].astype(F32), axis=0)
    tail = split_tail(join_tail(total[64:]))
    for k in range(out_ref.shape[0]):
        out_ref[k, :64, :] = total[:64].astype(BF16)
        out_ref[k, 64:, :] = tail

def final_kernel(parts_ref, w1_ref, w2_ref, b1_ref, loss_ref):
    total = jnp.sum(parts_ref[...].astype(F32), axis=0)
    tail = join_tail(total[64:])
    inverse = 1.0 / tail[1:2, REST + 1 : REST + 2]
    w1_ref[...] = total[:32] * inverse
    w2_ref[:, :TILE] = total[32:64] * inverse
    w2_ref[:16, TILE:] = tail[:, :REST] * inverse
    w2_ref[16:, TILE:] = pltpu.roll(tail, HALF, 1)[:, :REST] * inverse
    column = jnp.concatenate(
        [tail[:, REST : REST + 1], tail[:, HALF + REST : HALF + REST + 1]], axis=0
    )
    square = (32, 32)
    eye = lax.broadcasted_iota(jnp.int32, square, 0) == lax.broadcasted_iota(jnp.int32, square, 1)
    b1_ref[...] = jnp.sum(jnp.where(eye, column, 0.0), axis=0, keepdims=True) * inverse
    loss_ref[...] = tail[0:1, REST + 1 : REST + 2] * inverse

def on_device(
    features,
    weight_in,
    bias,
    weight_out,
    adj_tiles,
    tile_rows,
    tile_cols,
    tile_live,
    labels,
    label_mask,
):
    n_row, n_col = lax.axis_size("row"), lax.axis_size("col")
    n_core = lax.axis_size("core")
    n_feat = lax.axis_size("x") * n_core
    nodes, feats = features.shape
    row_blocks = nodes * n_col // TILE
    col_blocks = nodes * n_row // TILE
    grad_rows = 80

    x_mine = features.T
    x_other = lax.ppermute(x_mine, "core", [(0, 1), (1, 0)])
    x_pair = call(pair_kernel, pltpu.VMEM((2 * feats, nodes), BF16), x_mine, x_other)
    x_rows = [
        lax.ppermute(x_pair, "row", [(r, (r + k) % n_row) for r in range(n_row)])
        for k in range(1, n_row)
    ]
    tiles = adj_tiles.reshape(adj_tiles.shape[2:])
    loaded = pl.pallas_call(
        load_kernel,
        out_shape=pltpu.VMEM(tiles.shape, BF16),
        in_specs=[pl.BlockSpec(memory_space=pltpu.HBM)],
        out_specs=IN_VMEM,
        scratch_shapes=[pltpu.SemaphoreType.DMA((8,))],
        compiler_params=pltpu.CompilerParams(vmem_limit_bytes=2**20),
        cost_estimate=pl.CostEstimate(
            flops=0, bytes_accessed=4 * tiles.size, transcendentals=0
        ),
    )(pltpu.with_memory_space_constraint(tiles, pltpu.HBM))
    slots, weights = pl.pallas_call(
        setup_kernel,
        out_shape=(
            pltpu.VMEM((1, row_blocks // 2 * col_blocks), jnp.int32),
            pltpu.VMEM((96, TILE), BF16),
        ),
        in_specs=[IN_SMEM] + [IN_VMEM] * 5,
        out_specs=(IN_VMEM, IN_VMEM),
        compiler_params=pltpu.CompilerParams(vmem_limit_bytes=8 * 2**20),
    )(tile_live, tile_rows, tile_cols, weight_in.T, weight_out, bias.reshape(1, -1))
    partial = call(
        aggregate_kernel,
        pltpu.VMEM((n_col, 4 * feats, TILE), BF16),
        slots,
        x_pair,
        *x_rows,
        loaded,
        scalars=1,
        scratch=[pltpu.VMEM((2 * feats, n_row * nodes), BF16)],
    )
    parts = lax.all_to_all(partial, "col", 0, 0)
    rows = parts.shape[1] + weights.shape[0]
    message = call(total_kernel, pltpu.VMEM((n_feat, rows, TILE), BF16), parts, weights)
    gathered = lax.all_to_all(message, ("x", "core"), 0, 0)
    grads = call(
        node_kernel,
        pltpu.VMEM((n_row, grad_rows, TILE), BF16),
        gathered,
        weights,
        labels.reshape(1, -1),
        label_mask.reshape(1, -1),
        scratch=[pltpu.VMEM((feats * n_feat, nodes), BF16)],
    )
    grads = lax.all_to_all(grads, "row", 0, 0)
    grads = call(middle_kernel, pltpu.VMEM((n_col, grad_rows, TILE), BF16), grads)
    grads = lax.all_to_all(grads, "col", 0, 0)
    w1, w2, b1, loss = call(
        final_kernel,
        (
            jax.ShapeDtypeStruct((32, TILE), F32),
            jax.ShapeDtypeStruct((32, CLASSES), F32),
            jax.ShapeDtypeStruct((1, 32), F32),
            jax.ShapeDtypeStruct((1, 1), F32),
        ),
        grads,
    )
    return (loss.reshape(()), w1.T, b1.reshape(-1), w2)

def solution(mesh):
    shape = mesh.devices.shape
    split = jax.sharding.Mesh(
        mesh.devices.reshape(*shape[:2], shape[2] // 2, 2), ("row", "col", "x", "core")
    )
    feat = ("x", "core")
    in_specs = (
        P(("col", "row"), feat),
        P(None, feat),
        P(feat),
        P(feat, None),
        P("row", "col", None, None, None),
        P("row", "col", None),
        P("row", "col", None),
        P("row", "col"),
        P(("row", "col")),
        P(("row", "col")),
    )
    out_specs = (P(), P(None, feat), P(feat), P(feat, None))
    return jax.shard_map(
        on_device, mesh=split, in_specs=in_specs, out_specs=out_specs, check_vma=False
    )
```

```python
import functools

import jax
import jax.numpy as jnp
from jax import lax
from jax.experimental import pallas as pl
from jax.experimental.pallas import tpu as pltpu
from jax.sharding import PartitionSpec as P

CLASSES = 172
TILE = 128
REST = CLASSES - TILE
HALF = TILE // 2
GELU_SCALE = 0.7978845608028654
GELU_CUBE = 0.044715
LOAD_UNROLL = 16
F32 = jnp.float32
BF16 = jnp.bfloat16
IN_VMEM = pl.BlockSpec(memory_space=pltpu.VMEM)
IN_SMEM = pl.BlockSpec(memory_space=pltpu.SMEM)

def dot(a, b, contract=((1,), (0,))):
    return lax.dot_general(a, b, (contract, ((), ())), preferred_element_type=F32)

def gelu_parts(v):
    squared = v * v
    t = jnp.tanh(GELU_SCALE * v * (1.0 + GELU_CUBE * squared))
    return squared, t

def call(kernel, out_shape, *args, scalars=0, scratch=(), limit=16 * 2**20, cost=None):
    placed = args[:scalars] + tuple(
        pltpu.with_memory_space_constraint(arg, pltpu.VMEM) for arg in args[scalars:]
    )
    many = isinstance(out_shape, tuple)
    return pl.pallas_call(
        kernel,
        out_shape=out_shape,
        in_specs=[IN_SMEM] * scalars + [IN_VMEM] * (len(args) - scalars),
        out_specs=(IN_VMEM,) * len(out_shape) if many else IN_VMEM,
        scratch_shapes=scratch,
        compiler_params=pltpu.CompilerParams(vmem_limit_bytes=limit),
        cost_estimate=cost,
    )(*placed)

def load_kernel(place_ref, tiles_ref, after_ref, out_ref, sem):
    del after_ref
    slots = tiles_ref.shape[0]

    def start(trip, started):
        for part in range(LOAD_UNROLL):
            slot = trip * LOAD_UNROLL + part
            place = place_ref[0, slot]

            @pl.when(place >= 0)
            def _():
                pltpu.make_async_copy(tiles_ref.at[slot], out_ref.at[place], sem).start()

            started = started + (place >= 0).astype(jnp.int32)
        return started

    def finish(k, carry):
        pltpu.make_async_copy(tiles_ref.at[0], out_ref.at[0], sem).wait()
        return carry

    started = lax.fori_loop(0, slots // LOAD_UNROLL, start, 0)
    lax.fori_loop(0, started, finish, 0)


def pair_kernel(x_ref, other_ref, out_ref):
    first = lax.axis_index("core") == 0
    mine, other = x_ref[...], other_ref[...]
    feats = mine.shape[0]
    out_ref[:feats, :] = jnp.where(first, mine, other)
    out_ref[feats:, :] = jnp.where(first, other, mine)


def setup_kernel(
    live_ref, rows_in, cols_in, w1_in, w2_in, bias_in, x_in,
    place_ref, used_ref, weights_ref, x_ref, rows_ref, cols_ref, w1_ref, w2_ref, bias_ref, sems,
):
    sources = (rows_in, cols_in, w1_in, w2_in, bias_in, x_in)
    targets = (rows_ref, cols_ref, w1_ref, w2_ref, bias_ref, x_ref)
    copies = [
        pltpu.make_async_copy(source, target, sems.at[k])
        for k, (source, target) in enumerate(zip(sources, targets))
    ]
    for copy in copies:
        copy.start()
    for copy in copies:
        copy.wait()
    place_tiles(live_ref, rows_ref, cols_ref, place_ref, used_ref)
    pack_weights(w1_ref, w2_ref, bias_ref, weights_ref)


def place_tiles(live_ref, rows_ref, cols_ref, place_ref, used_ref):
    places = used_ref.shape[1]
    slots = rows_ref.shape[2]
    slot = lax.broadcasted_iota(jnp.int32, (1, slots), 1)
    rows = rows_ref[0]
    place = ((rows >> 2) * 2 + (rows & 1)) * (places // 16) + cols_ref[0]
    mine = (slot < live_ref[0, 0]) & (((rows >> 1) & 1) == lax.axis_index("core"))
    place = jnp.where(mine, place, -1)
    place_ref[...] = place
    here = lax.broadcasted_iota(jnp.int32, (places, slots), 0) == place
    onehot = jnp.where(here, 1.0, 0.0).astype(BF16)
    used = dot(jnp.ones((8, slots), BF16), onehot, ((1,), (1,)))
    used_ref[...] = used[0:1].astype(jnp.int32)


def aggregate_kernel(used_ref, x0_ref, x1_ref, x2_ref, x3_ref, tiles_ref, out_ref, all_ref):
    feats, nodes = x0_ref.shape
    row, n_row = lax.axis_index("row"), lax.axis_size("row")
    for k, part in enumerate((x0_ref, x1_ref, x2_ref, x3_ref)):
        source = lax.rem(row + n_row - k, n_row)
        all_ref[:, pl.ds(pl.multiple_of(source * nodes, TILE), nodes)] = part[...]
    x_all = all_ref[...]
    groups = out_ref.shape[0]
    col_blocks = used_ref.shape[1] // (2 * groups)
    for group in range(groups):
        strips = []
        for block in (2 * group, 2 * group + 1):
            tiles = []
            for j in range(col_blocks):
                place = block * col_blocks + j
                tile = tiles_ref[place]
                tiles.append(jnp.where(used_ref[0, place] > 0, tile, jnp.zeros_like(tile)))
            strips.append(jnp.concatenate(tiles, 1))
        wide = dot(x_all, jnp.concatenate(strips, 0), ((1,), (1,))).astype(BF16)
        out_ref[group, :feats, :] = wide[:, :TILE]
        out_ref[group, feats:, :] = wide[:, TILE:]


def pack_weights(w1_ref, w2_ref, bias_ref, out_ref):
    shape = (32, TILE)
    lane = lax.broadcasted_iota(jnp.int32, shape, 1)
    sub = lax.broadcasted_iota(jnp.int32, shape, 0)
    row = jnp.concatenate([bias_ref[...], jnp.zeros((1, TILE - 32), F32)], axis=1)
    bias = jnp.sum(jnp.where(lane == sub, row, 0.0), axis=1, keepdims=True)
    high = bias.astype(BF16).astype(F32)
    middle = (bias - high).astype(BF16).astype(F32)
    low = bias - high - middle
    rest = jnp.concatenate(
        [w2_ref[:, TILE:].astype(F32), jnp.zeros((32, TILE - REST), F32)], axis=1
    )
    for place, part in ((REST, high), (REST + 1, middle), (REST + 2, low)):
        rest = jnp.where(lane == place, part, rest)
    out_ref[:32, :] = w1_ref[...]
    out_ref[32:64, :] = w2_ref[:, :TILE]
    out_ref[64:, :] = rest.astype(BF16)

def total_kernel(parts_ref, weights_ref, out_ref):
    total = jnp.sum(parts_ref[...].astype(F32), axis=0).astype(BF16)
    rows = total.shape[0]
    out_ref[:rows, :] = total
    out_ref[rows:, :] = weights_ref[...]


def stack_kernel(*refs):
    for k, part in enumerate(refs[:-1]):
        refs[-1][k] = part[...]


def lanes16():
    return lax.broadcasted_iota(jnp.int32, (16, TILE), 1)

def is_fine(lane):
    return (lane == REST) | (lane == REST + 1) | (lane == HALF + REST)

def split_tail(tail):
    upper = tail.astype(BF16).astype(F32)
    moved = pltpu.roll(tail - upper, 2, 1)
    return jnp.where(is_fine(lanes16() - 2), moved, upper).astype(BF16)

def join_tail(tail):
    return jnp.where(is_fine(lanes16()), tail + pltpu.roll(tail, TILE - 2, 1), tail)

def node_kernel(mine_ref, other_ref, labels_ref, mask_ref, out_ref, y_ref):
    n_x = mine_ref.shape[0]
    x, core = lax.axis_index("x"), lax.axis_index("core")
    for ref, owner in ((mine_ref, core), (other_ref, 1 - core)):
        for k in range(n_x):
            feat = pl.multiple_of(lax.rem(x + n_x - k, n_x) * 32, 32)
            for b in range(2):
                node = pl.multiple_of((2 * owner + b) * TILE, TILE)
                y_ref[pl.ds(feat, 32), pl.ds(node, TILE)] = ref[k, 32 * b : 32 * b + 32, :]
    y = y_ref[...]

    def both(begin):
        rows = 32 * n_x
        return jnp.concatenate(
            [ref[:, begin : begin + 32, :].reshape(rows, TILE) for ref in (mine_ref, other_ref)], 0
        )

    w1, w2a, w2b = both(64), both(96), both(128)

    def bias_of(block):
        wide = block.astype(F32)
        return wide[:, REST : REST + 1] + wide[:, REST + 1 : REST + 2] + wide[:, REST + 2 : REST + 3]

    preact = dot(w1, y) + bias_of(w2b)
    _, t = gelu_parts(preact)
    hidden = (0.5 * preact * (1.0 + t)).astype(BF16)
    logits_a = dot(w2a, hidden, ((0,), (0,)))
    logits_b = dot(w2b, hidden, ((0,), (0,)))[:48]
    labels = labels_ref[...]
    mask = mask_ref[...].astype(F32)
    class_a = lax.broadcasted_iota(jnp.int32, logits_a.shape, 0)
    class_b = lax.broadcasted_iota(jnp.int32, logits_b.shape, 0) + TILE
    logits_b = jnp.where(class_b < CLASSES, logits_b, -jnp.inf)
    top = jnp.maximum(
        jnp.max(logits_a, axis=0, keepdims=True), jnp.max(logits_b, axis=0, keepdims=True)
    )
    shifted_a = logits_a - top
    shifted_b = logits_b - top
    exp_a = jnp.exp(shifted_a)
    exp_b = jnp.exp(shifted_b)
    expsum = jnp.sum(exp_a, axis=0, keepdims=True) + jnp.sum(exp_b, axis=0, keepdims=True)
    hit_a = class_a == labels
    hit_b = class_b == labels
    picked = jnp.sum(jnp.where(hit_a, shifted_a, 0.0), axis=0, keepdims=True) + jnp.sum(
        jnp.where(hit_b, shifted_b, 0.0), axis=0, keepdims=True
    )
    loss = jnp.sum((jnp.log(expsum) - picked) * mask)
    count = jnp.sum(mask)
    inverse = 1.0 / expsum
    grad_a = ((exp_a * inverse - hit_a.astype(F32)) * mask).astype(BF16)
    grad_b = ((exp_b * inverse - hit_b.astype(F32)) * mask).astype(BF16)

    own_w1 = mine_ref[0, 64:96, :]
    own_w2a = mine_ref[0, 96:128, :]
    own_w2b = mine_ref[0, 128:, :]
    own_pre = dot(own_w1, y) + bias_of(own_w2b)
    squared, own_t = gelu_parts(own_pre)
    own_hidden = (0.5 * own_pre * (1.0 + own_t)).astype(BF16)
    slope = 0.5 * (1.0 + own_t) + 0.5 * own_pre * (1.0 - own_t * own_t) * (
        GELU_SCALE * (1.0 + 3.0 * GELU_CUBE * squared)
    )
    grad_hidden = dot(own_w2a, grad_a) + dot(own_w2b[:, :48], grad_b)
    grad_pre = (grad_hidden * slope).astype(BF16)
    grad_b1 = jnp.sum(grad_pre.astype(F32), axis=1, keepdims=True)
    grad_w1 = dot(grad_pre, y, ((1,), (1,))).astype(BF16)
    grad_w2a = dot(own_hidden, grad_a, ((1,), (1,))).astype(BF16)
    grad_w2b = dot(own_hidden, grad_b, ((1,), (1,)))
    lane = lanes16()
    sub = lax.broadcasted_iota(jnp.int32, lane.shape, 0)
    wide = jnp.concatenate([grad_w2b, jnp.zeros((32, TILE - 48), F32)], axis=1)
    extra = jnp.where(sub == 0, loss, jnp.where(sub == 1, count, 0.0))
    tail = jnp.where(lane < HALF, wide[:16], pltpu.roll(wide[16:], HALF, 1))
    tail = jnp.where(lane == REST, grad_b1[:16], tail)
    tail = jnp.where(lane == REST + 1, extra, tail)
    tail = jnp.where(lane == HALF + REST, grad_b1[16:], tail)
    tail = split_tail(tail)
    out_ref[:32, :] = grad_w1
    out_ref[32:64, :] = grad_w2a
    out_ref[64:, :] = tail


def middle_kernel(*refs):
    out_ref = refs[-1]
    total = sum(part[...].astype(F32) for part in refs[:-1])
    tail = split_tail(join_tail(total[64:]))
    for k in range(out_ref.shape[0]):
        out_ref[k, :64, :] = total[:64].astype(BF16)
        out_ref[k, 64:, :] = tail

def final_kernel(parts_ref, w1_ref, w2_ref, b1_ref, loss_ref):
    total = jnp.sum(parts_ref[...].astype(F32), axis=0)
    tail = join_tail(total[64:])
    inverse = 1.0 / tail[1:2, REST + 1 : REST + 2]
    w1_ref[...] = total[:32] * inverse
    w2_ref[:, :TILE] = total[32:64] * inverse
    w2_ref[:16, TILE:] = tail[:, :REST] * inverse
    w2_ref[16:, TILE:] = pltpu.roll(tail, HALF, 1)[:, :REST] * inverse
    column = jnp.concatenate(
        [tail[:, REST : REST + 1], tail[:, HALF + REST : HALF + REST + 1]], axis=0
    )
    square = (32, 32)
    eye = lax.broadcasted_iota(jnp.int32, square, 0) == lax.broadcasted_iota(jnp.int32, square, 1)
    b1_ref[...] = jnp.sum(jnp.where(eye, column, 0.0), axis=0, keepdims=True) * inverse
    loss_ref[...] = tail[0:1, REST + 1 : REST + 2] * inverse

def shifted(value, axis):
    size = lax.axis_size(axis)
    return [
        lax.ppermute(value, axis, [(k, (k + step) % size) for k in range(size)])
        for step in range(1, size)
    ]


def on_device(
    features,
    weight_in,
    bias,
    weight_out,
    adj_tiles,
    tile_rows,
    tile_cols,
    tile_live,
    labels,
    label_mask,
):
    n_row, n_col = lax.axis_size("row"), lax.axis_size("col")
    n_core = lax.axis_size("core")
    n_feat = lax.axis_size("x") * n_core
    nodes, feats = features.shape
    row_blocks = nodes * n_col // TILE
    col_blocks = nodes * n_row // TILE
    grad_rows = 80

    x_mine = features.T
    x_other = lax.ppermute(x_mine, "core", [(0, 1), (1, 0)])
    tiles = pltpu.with_memory_space_constraint(
        adj_tiles.reshape(adj_tiles.shape[2:]), pltpu.HBM
    )
    places = row_blocks // 2 * col_blocks
    small = (tile_rows, tile_cols, weight_in.T, weight_out, bias.reshape(1, -1), x_mine)
    place, used, weights, x_mine = pl.pallas_call(
        setup_kernel,
        out_shape=(
            pltpu.VMEM((1, tiles.shape[0]), jnp.int32),
            pltpu.VMEM((1, places), jnp.int32),
            pltpu.VMEM((96, TILE), BF16),
            pltpu.VMEM(x_mine.shape, BF16),
        ),
        in_specs=[IN_SMEM] + [pl.BlockSpec(memory_space=pltpu.HBM)] * 6,
        out_specs=(IN_VMEM,) * 4,
        scratch_shapes=[pltpu.VMEM(v.shape, v.dtype) for v in small[:5]]
        + [pltpu.SemaphoreType.DMA((6,))],
        compiler_params=pltpu.CompilerParams(vmem_limit_bytes=8 * 2**20),
    )(tile_live, *(pltpu.with_memory_space_constraint(v, pltpu.HBM) for v in small))
    x_pair = call(pair_kernel, pltpu.VMEM((2 * feats, nodes), BF16), x_mine, x_other)
    x_rows = shifted(x_pair, "row")
    loaded = pl.pallas_call(
        load_kernel,
        out_shape=pltpu.VMEM((places, TILE, TILE), BF16),
        in_specs=[IN_SMEM, pl.BlockSpec(memory_space=pltpu.HBM), IN_VMEM],
        out_specs=IN_VMEM,
        scratch_shapes=[pltpu.SemaphoreType.DMA],
        compiler_params=pltpu.CompilerParams(vmem_limit_bytes=2**20),
        cost_estimate=pl.CostEstimate(
            flops=0, bytes_accessed=2 * tiles.size, transcendentals=0
        ),
    )(place, tiles, pltpu.with_memory_space_constraint(x_pair, pltpu.VMEM))
    partial = call(
        aggregate_kernel,
        pltpu.VMEM((n_col, 4 * feats, TILE), BF16),
        used,
        x_pair,
        *x_rows,
        loaded,
        scalars=1,
        scratch=[pltpu.VMEM((2 * feats, n_row * nodes), BF16)],
    )
    parts = lax.all_to_all(partial, "col", 0, 0)
    rows = parts.shape[1] + weights.shape[0]
    message = call(total_kernel, pltpu.VMEM((rows, TILE), BF16), parts, weights)
    messages = (message, *shifted(message, "x"))
    mine = call(stack_kernel, pltpu.VMEM((len(messages), rows, TILE), BF16), *messages)
    other = lax.ppermute(mine, "core", [(0, 1), (1, 0)])
    grads = call(
        node_kernel,
        pltpu.VMEM((grad_rows, TILE), BF16),
        mine,
        other,
        labels.reshape(1, -1),
        label_mask.reshape(1, -1),
        scratch=[pltpu.VMEM((feats * n_feat, nodes), BF16)],
    )
    grads = call(
        middle_kernel,
        pltpu.VMEM((n_col, grad_rows, TILE), BF16),
        grads,
        *shifted(grads, "row"),
    )
    grads = lax.all_to_all(grads, "col", 0, 0)
    w1, w2, b1, loss = call(
        final_kernel,
        (
            jax.ShapeDtypeStruct((32, TILE), F32),
            jax.ShapeDtypeStruct((32, CLASSES), F32),
            jax.ShapeDtypeStruct((1, 32), F32),
            jax.ShapeDtypeStruct((1, 1), F32),
        ),
        grads,
    )
    return (loss.reshape(()), w1.T, b1.reshape(-1), w2)

def solution(mesh):
    shape = mesh.devices.shape
    split = jax.sharding.Mesh(
        mesh.devices.reshape(*shape[:2], shape[2] // 2, 2), ("row", "col", "x", "core")
    )
    feat = ("x", "core")
    in_specs = (
        P(("col", "row"), feat),
        P(None, feat),
        P(feat),
        P(feat, None),
        P("row", "col", None, None, None),
        P("row", "col", None),
        P("row", "col", None),
        P("row", "col"),
        P(("row", "col")),
        P(("row", "col")),
    )
    out_specs = (P(), P(None, feat), P(feat), P(feat, None))
    return jax.shard_map(
        on_device, mesh=split, in_specs=in_specs, out_specs=out_specs, check_vma=False
    )
```

```python
import functools

import jax
import jax.numpy as jnp
from jax import lax
from jax.experimental import pallas as pl
from jax.experimental.pallas import tpu as pltpu
from jax.sharding import PartitionSpec as P

CLASSES = 172
TILE = 128
REST = CLASSES - TILE
HALF = TILE // 2
GELU_SCALE = 0.7978845608028654
GELU_CUBE = 0.044715
LOAD_UNROLL = 16
ORDER = (1, 3, 2)
F32 = jnp.float32
BF16 = jnp.bfloat16
IN_VMEM = pl.BlockSpec(memory_space=pltpu.VMEM)
IN_SMEM = pl.BlockSpec(memory_space=pltpu.SMEM)

def dot(a, b, contract=((1,), (0,))):
    return lax.dot_general(a, b, (contract, ((), ())), preferred_element_type=F32)

def gelu_parts(v):
    squared = v * v
    t = jnp.tanh(GELU_SCALE * v * (1.0 + GELU_CUBE * squared))
    return squared, t

def call(kernel, out_shape, *args, scalars=0, scratch=(), limit=16 * 2**20, cost=None):
    placed = args[:scalars] + tuple(
        pltpu.with_memory_space_constraint(arg, pltpu.VMEM) for arg in args[scalars:]
    )
    many = isinstance(out_shape, tuple)
    return pl.pallas_call(
        kernel,
        out_shape=out_shape,
        in_specs=[IN_SMEM] * scalars + [IN_VMEM] * (len(args) - scalars),
        out_specs=(IN_VMEM,) * len(out_shape) if many else IN_VMEM,
        scratch_shapes=scratch,
        compiler_params=pltpu.CompilerParams(vmem_limit_bytes=limit),
        cost_estimate=cost,
    )(*placed)

def load_kernel(place_ref, tiles_ref, after_ref, out_ref, sem):
    del after_ref
    slots = tiles_ref.shape[0]

    def start(trip, started):
        for part in range(LOAD_UNROLL):
            slot = trip * LOAD_UNROLL + part
            place = place_ref[0, slot]

            @pl.when(place >= 0)
            def _():
                pltpu.make_async_copy(tiles_ref.at[slot], out_ref.at[place], sem).start()

            started = started + (place >= 0).astype(jnp.int32)
        return started

    def finish(k, carry):
        pltpu.make_async_copy(tiles_ref.at[0], out_ref.at[0], sem).wait()
        return carry

    started = lax.fori_loop(0, slots // LOAD_UNROLL, start, 0)
    lax.fori_loop(0, started, finish, 0)


def pair_kernel(x_ref, other_ref, out_ref):
    first = lax.axis_index("core") == 0
    mine, other = x_ref[...], other_ref[...]
    feats = mine.shape[0]
    out_ref[:feats, :] = jnp.where(first, mine, other)
    out_ref[feats:, :] = jnp.where(first, other, mine)


def setup_kernel(
    live_ref, rows_in, cols_in, w1_in, w2_in, bias_in, x_in,
    place_ref, used_ref, weights_ref, x_ref, rows_ref, cols_ref, w1_ref, w2_ref, bias_ref, sems,
):
    sources = (rows_in, cols_in, w1_in, w2_in, bias_in, x_in)
    targets = (rows_ref, cols_ref, w1_ref, w2_ref, bias_ref, x_ref)
    copies = [
        pltpu.make_async_copy(source, target, sems.at[k])
        for k, (source, target) in enumerate(zip(sources, targets))
    ]
    for copy in copies:
        copy.start()
    for copy in copies:
        copy.wait()
    place_tiles(live_ref, rows_ref, cols_ref, place_ref, used_ref)
    pack_weights(w1_ref, w2_ref, bias_ref, weights_ref)


def place_tiles(live_ref, rows_ref, cols_ref, place_ref, used_ref):
    places = used_ref.shape[1]
    slots = rows_ref.shape[2]
    slot = lax.broadcasted_iota(jnp.int32, (1, slots), 1)
    rows = rows_ref[0]
    place = ((rows >> 2) * 2 + (rows & 1)) * (places // 16) + cols_ref[0]
    mine = (slot < live_ref[0, 0]) & (((rows >> 1) & 1) == lax.axis_index("core"))
    place = jnp.where(mine, place, -1)
    place_ref[...] = place
    here = lax.broadcasted_iota(jnp.int32, (places, slots), 0) == place
    onehot = jnp.where(here, 1.0, 0.0).astype(BF16)
    used = dot(jnp.ones((8, slots), BF16), onehot, ((1,), (1,)))
    used_ref[...] = used[0:1].astype(jnp.int32)


def aggregate_kernel(used_ref, x0_ref, x1_ref, x2_ref, x3_ref, tiles_ref, out_ref, all_ref):
    feats, nodes = x0_ref.shape
    row, n_row = lax.axis_index("row"), lax.axis_size("row")
    for k, part in zip((0, *ORDER), (x0_ref, x1_ref, x2_ref, x3_ref)):
        source = row ^ k
        all_ref[:, pl.ds(pl.multiple_of(source * nodes, TILE), nodes)] = part[...]
    x_all = all_ref[...]
    groups = out_ref.shape[0]
    col_blocks = used_ref.shape[1] // (2 * groups)
    for group in range(groups):
        strips = []
        for block in (2 * group, 2 * group + 1):
            tiles = []
            for j in range(col_blocks):
                place = block * col_blocks + j
                tile = tiles_ref[place]
                tiles.append(jnp.where(used_ref[0, place] > 0, tile, jnp.zeros_like(tile)))
            strips.append(jnp.concatenate(tiles, 1))
        wide = dot(jnp.concatenate(strips, 0), x_all, ((1,), (1,))).T.astype(BF16)
        out_ref[group, :feats, :] = wide[:, :TILE]
        out_ref[group, feats:, :] = wide[:, TILE:]


def pack_weights(w1_ref, w2_ref, bias_ref, out_ref):
    shape = (32, TILE)
    lane = lax.broadcasted_iota(jnp.int32, shape, 1)
    sub = lax.broadcasted_iota(jnp.int32, shape, 0)
    row = jnp.concatenate([bias_ref[...], jnp.zeros((1, TILE - 32), F32)], axis=1)
    bias = jnp.sum(jnp.where(lane == sub, row, 0.0), axis=1, keepdims=True)
    high = bias.astype(BF16).astype(F32)
    middle = (bias - high).astype(BF16).astype(F32)
    low = bias - high - middle
    rest = jnp.concatenate(
        [w2_ref[:, TILE:].astype(F32), jnp.zeros((32, TILE - REST), F32)], axis=1
    )
    for place, part in ((REST, high), (REST + 1, middle), (REST + 2, low)):
        rest = jnp.where(lane == place, part, rest)
    out_ref[:32, :] = w1_ref[...]
    out_ref[32:64, :] = w2_ref[:, :TILE]
    out_ref[64:, :] = rest.astype(BF16)

def total_kernel(parts_ref, weights_ref, out_ref):
    total = jnp.sum(parts_ref[...].astype(F32), axis=0).astype(BF16)
    rows = total.shape[0]
    out_ref[:rows, :] = total
    out_ref[rows:, :] = weights_ref[...]


def stack_kernel(*refs):
    for k, part in zip((0, *ORDER), refs[:-1]):
        refs[-1][k] = part[...]


def lanes16():
    return lax.broadcasted_iota(jnp.int32, (16, TILE), 1)

def is_fine(lane):
    return (lane == REST) | (lane == REST + 1) | (lane == HALF + REST)

def split_tail(tail):
    upper = tail.astype(BF16).astype(F32)
    moved = pltpu.roll(tail - upper, 2, 1)
    return jnp.where(is_fine(lanes16() - 2), moved, upper).astype(BF16)

def join_tail(tail):
    return jnp.where(is_fine(lanes16()), tail + pltpu.roll(tail, TILE - 2, 1), tail)

def node_kernel(mine_ref, other_ref, labels_ref, mask_ref, out_ref, y_ref):
    n_x = mine_ref.shape[0]
    x, core = lax.axis_index("x"), lax.axis_index("core")
    for ref, owner in ((mine_ref, core), (other_ref, 1 - core)):
        for k in range(n_x):
            feat = pl.multiple_of((x ^ k) * 32, 32)
            for b in range(2):
                node = pl.multiple_of((2 * owner + b) * TILE, TILE)
                y_ref[pl.ds(feat, 32), pl.ds(node, TILE)] = ref[k, 32 * b : 32 * b + 32, :]
    y = y_ref[...]

    def both(begin):
        rows = 32 * n_x
        return jnp.concatenate(
            [ref[:, begin : begin + 32, :].reshape(rows, TILE) for ref in (mine_ref, other_ref)], 0
        )

    w1, w2a, w2b = both(64), both(96), both(128)

    def bias_of(block):
        wide = block.astype(F32)
        return wide[:, REST : REST + 1] + wide[:, REST + 1 : REST + 2] + wide[:, REST + 2 : REST + 3]

    preact = dot(w1, y) + bias_of(w2b)
    _, t = gelu_parts(preact)
    hidden = (0.5 * preact * (1.0 + t)).astype(BF16)
    logits_a = dot(w2a, hidden, ((0,), (0,)))
    logits_b = dot(w2b, hidden, ((0,), (0,)))[:48]
    labels = labels_ref[...]
    mask = mask_ref[...].astype(F32)
    class_a = lax.broadcasted_iota(jnp.int32, logits_a.shape, 0)
    class_b = lax.broadcasted_iota(jnp.int32, logits_b.shape, 0) + TILE
    logits_b = jnp.where(class_b < CLASSES, logits_b, -jnp.inf)
    top = jnp.maximum(
        jnp.max(logits_a, axis=0, keepdims=True), jnp.max(logits_b, axis=0, keepdims=True)
    )
    shifted_a = logits_a - top
    shifted_b = logits_b - top
    exp_a = jnp.exp(shifted_a)
    exp_b = jnp.exp(shifted_b)
    expsum = jnp.sum(exp_a, axis=0, keepdims=True) + jnp.sum(exp_b, axis=0, keepdims=True)
    hit_a = class_a == labels
    hit_b = class_b == labels
    picked = jnp.sum(jnp.where(hit_a, shifted_a, 0.0), axis=0, keepdims=True) + jnp.sum(
        jnp.where(hit_b, shifted_b, 0.0), axis=0, keepdims=True
    )
    loss = jnp.sum((jnp.log(expsum) - picked) * mask)
    count = jnp.sum(mask)
    inverse = 1.0 / expsum
    grad_a = ((exp_a * inverse - hit_a.astype(F32)) * mask).astype(BF16)
    grad_b = ((exp_b * inverse - hit_b.astype(F32)) * mask).astype(BF16)

    own_w1 = mine_ref[0, 64:96, :]
    own_w2a = mine_ref[0, 96:128, :]
    own_w2b = mine_ref[0, 128:, :]
    own_pre = dot(own_w1, y) + bias_of(own_w2b)
    squared, own_t = gelu_parts(own_pre)
    own_hidden = (0.5 * own_pre * (1.0 + own_t)).astype(BF16)
    slope = 0.5 * (1.0 + own_t) + 0.5 * own_pre * (1.0 - own_t * own_t) * (
        GELU_SCALE * (1.0 + 3.0 * GELU_CUBE * squared)
    )
    grad_hidden = dot(own_w2a, grad_a) + dot(own_w2b[:, :48], grad_b)
    grad_pre = (grad_hidden * slope).astype(BF16)
    grad_b1 = jnp.sum(grad_pre.astype(F32), axis=1, keepdims=True)
    grad_w1 = dot(grad_pre, y, ((1,), (1,))).astype(BF16)
    grad_w2a = dot(own_hidden, grad_a, ((1,), (1,))).astype(BF16)
    grad_w2b = dot(own_hidden, grad_b, ((1,), (1,)))
    lane = lanes16()
    sub = lax.broadcasted_iota(jnp.int32, lane.shape, 0)
    wide = jnp.concatenate([grad_w2b, jnp.zeros((32, TILE - 48), F32)], axis=1)
    extra = jnp.where(sub == 0, loss, jnp.where(sub == 1, count, 0.0))
    tail = jnp.where(lane < HALF, wide[:16], pltpu.roll(wide[16:], HALF, 1))
    tail = jnp.where(lane == REST, grad_b1[:16], tail)
    tail = jnp.where(lane == REST + 1, extra, tail)
    tail = jnp.where(lane == HALF + REST, grad_b1[16:], tail)
    tail = split_tail(tail)
    out_ref[:32, :] = grad_w1
    out_ref[32:64, :] = grad_w2a
    out_ref[64:, :] = tail


def middle_kernel(*refs):
    out_ref = refs[-1]
    total = sum(part[...].astype(F32) for part in refs[:-1])
    tail = split_tail(join_tail(total[64:]))
    for k in range(out_ref.shape[0]):
        out_ref[k, :64, :] = total[:64].astype(BF16)
        out_ref[k, 64:, :] = tail

def final_kernel(parts_ref, w1_ref, w2_ref, b1_ref, loss_ref):
    total = jnp.sum(parts_ref[...].astype(F32), axis=0)
    tail = join_tail(total[64:])
    inverse = 1.0 / tail[1:2, REST + 1 : REST + 2]
    w1_ref[...] = total[:32] * inverse
    w2_ref[:, :TILE] = total[32:64] * inverse
    w2_ref[:16, TILE:] = tail[:, :REST] * inverse
    w2_ref[16:, TILE:] = pltpu.roll(tail, HALF, 1)[:, :REST] * inverse
    column = jnp.concatenate(
        [tail[:, REST : REST + 1], tail[:, HALF + REST : HALF + REST + 1]], axis=0
    )
    square = (32, 32)
    eye = lax.broadcasted_iota(jnp.int32, square, 0) == lax.broadcasted_iota(jnp.int32, square, 1)
    b1_ref[...] = jnp.sum(jnp.where(eye, column, 0.0), axis=0, keepdims=True) * inverse
    loss_ref[...] = tail[0:1, REST + 1 : REST + 2] * inverse

def exchanged(value, axis):
    size = lax.axis_size(axis)
    return [
        lax.ppermute(value, axis, [(k, k ^ step) for k in range(size)])
        for step in ORDER
    ]


def on_device(
    features,
    weight_in,
    bias,
    weight_out,
    adj_tiles,
    tile_rows,
    tile_cols,
    tile_live,
    labels,
    label_mask,
):
    n_row, n_col = lax.axis_size("row"), lax.axis_size("col")
    n_core = lax.axis_size("core")
    n_feat = lax.axis_size("x") * n_core
    nodes, feats = features.shape
    row_blocks = nodes * n_col // TILE
    col_blocks = nodes * n_row // TILE
    grad_rows = 80

    x_mine = features.T
    x_other = lax.ppermute(x_mine, "core", [(0, 1), (1, 0)])
    tiles = pltpu.with_memory_space_constraint(
        adj_tiles.reshape(adj_tiles.shape[2:]), pltpu.HBM
    )
    places = row_blocks // 2 * col_blocks
    small = (tile_rows, tile_cols, weight_in.T, weight_out, bias.reshape(1, -1), x_mine)
    place, used, weights, x_mine = pl.pallas_call(
        setup_kernel,
        out_shape=(
            pltpu.VMEM((1, tiles.shape[0]), jnp.int32),
            pltpu.VMEM((1, places), jnp.int32),
            pltpu.VMEM((96, TILE), BF16),
            pltpu.VMEM(x_mine.shape, BF16),
        ),
        in_specs=[IN_SMEM] + [pl.BlockSpec(memory_space=pltpu.HBM)] * 6,
        out_specs=(IN_VMEM,) * 4,
        scratch_shapes=[pltpu.VMEM(v.shape, v.dtype) for v in small[:5]]
        + [pltpu.SemaphoreType.DMA((6,))],
        compiler_params=pltpu.CompilerParams(vmem_limit_bytes=8 * 2**20),
    )(tile_live, *(pltpu.with_memory_space_constraint(v, pltpu.HBM) for v in small))
    x_pair = call(pair_kernel, pltpu.VMEM((2 * feats, nodes), BF16), x_mine, x_other)
    x_rows = exchanged(x_pair, "row")
    loaded = pl.pallas_call(
        load_kernel,
        out_shape=pltpu.VMEM((places, TILE, TILE), BF16),
        in_specs=[IN_SMEM, pl.BlockSpec(memory_space=pltpu.HBM), IN_VMEM],
        out_specs=IN_VMEM,
        scratch_shapes=[pltpu.SemaphoreType.DMA],
        compiler_params=pltpu.CompilerParams(vmem_limit_bytes=2**20),
        cost_estimate=pl.CostEstimate(
            flops=0, bytes_accessed=2 * tiles.size, transcendentals=0
        ),
    )(place, tiles, pltpu.with_memory_space_constraint(x_pair, pltpu.VMEM))
    partial = call(
        aggregate_kernel,
        pltpu.VMEM((n_col, 4 * feats, TILE), BF16),
        used,
        x_pair,
        *x_rows,
        loaded,
        scalars=1,
        scratch=[pltpu.VMEM((2 * feats, n_row * nodes), BF16)],
    )
    parts = lax.all_to_all(partial, "col", 0, 0)
    rows = parts.shape[1] + weights.shape[0]
    message = call(total_kernel, pltpu.VMEM((rows, TILE), BF16), parts, weights)
    messages = (message, *exchanged(message, "x"))
    mine = call(stack_kernel, pltpu.VMEM((len(messages), rows, TILE), BF16), *messages)
    other = lax.ppermute(mine, "core", [(0, 1), (1, 0)])
    grads = call(
        node_kernel,
        pltpu.VMEM((grad_rows, TILE), BF16),
        mine,
        other,
        labels.reshape(1, -1),
        label_mask.reshape(1, -1),
        scratch=[pltpu.VMEM((feats * n_feat, nodes), BF16)],
    )
    grads = call(
        middle_kernel,
        pltpu.VMEM((n_col, grad_rows, TILE), BF16),
        grads,
        *exchanged(grads, "row"),
    )
    grads = lax.all_to_all(grads, "col", 0, 0)
    w1, w2, b1, loss = call(
        final_kernel,
        (
            jax.ShapeDtypeStruct((32, TILE), F32),
            jax.ShapeDtypeStruct((32, CLASSES), F32),
            jax.ShapeDtypeStruct((1, 32), F32),
            jax.ShapeDtypeStruct((1, 1), F32),
        ),
        grads,
    )
    return (loss.reshape(()), w1.T, b1.reshape(-1), w2)

def solution(mesh):
    shape = mesh.devices.shape
    split = jax.sharding.Mesh(
        mesh.devices.reshape(*shape[:2], shape[2] // 2, 2), ("row", "col", "x", "core")
    )
    feat = ("x", "core")
    in_specs = (
        P(("col", "row"), feat),
        P(None, feat),
        P(feat),
        P(feat, None),
        P("row", "col", None, None, None),
        P("row", "col", None),
        P("row", "col", None),
        P("row", "col"),
        P(("row", "col")),
        P(("row", "col")),
    )
    out_specs = (P(), P(None, feat), P(feat), P(feat, None))
    return jax.shard_map(
        on_device, mesh=split, in_specs=in_specs, out_specs=out_specs, check_vma=False
    )
```

```python
import functools

import jax
import jax.numpy as jnp
from jax import lax
from jax.experimental import pallas as pl
from jax.experimental.pallas import tpu as pltpu
from jax.sharding import PartitionSpec as P

CLASSES = 172
TILE = 128
REST = CLASSES - TILE
HALF = TILE // 2
GELU_SCALE = 0.7978845608028654
GELU_CUBE = 0.044715
LOAD_UNROLL = 16
COL_BITS = ("c0", "c1", "c2")
ORDER = (1, 3, 2)
F32 = jnp.float32
BF16 = jnp.bfloat16
IN_VMEM = pl.BlockSpec(memory_space=pltpu.VMEM)
IN_SMEM = pl.BlockSpec(memory_space=pltpu.SMEM)

def dot(a, b, contract=((1,), (0,))):
    return lax.dot_general(a, b, (contract, ((), ())), preferred_element_type=F32)

def gelu_parts(v):
    squared = v * v
    t = jnp.tanh(GELU_SCALE * v * (1.0 + GELU_CUBE * squared))
    return squared, t

def call(kernel, out_shape, *args, scalars=0, scratch=(), limit=16 * 2**20, cost=None):
    placed = args[:scalars] + tuple(
        pltpu.with_memory_space_constraint(arg, pltpu.VMEM) for arg in args[scalars:]
    )
    many = isinstance(out_shape, tuple)
    return pl.pallas_call(
        kernel,
        out_shape=out_shape,
        in_specs=[IN_SMEM] * scalars + [IN_VMEM] * (len(args) - scalars),
        out_specs=(IN_VMEM,) * len(out_shape) if many else IN_VMEM,
        scratch_shapes=scratch,
        compiler_params=pltpu.CompilerParams(vmem_limit_bytes=limit),
        cost_estimate=cost,
    )(*placed)

def load_kernel(place_ref, tiles_ref, after_ref, out_ref, sem):
    del after_ref
    slots = tiles_ref.shape[0]

    def start(trip, started):
        for part in range(LOAD_UNROLL):
            slot = trip * LOAD_UNROLL + part
            place = place_ref[0, slot]

            @pl.when(place >= 0)
            def _():
                pltpu.make_async_copy(tiles_ref.at[slot], out_ref.at[place], sem).start()

            started = started + (place >= 0).astype(jnp.int32)
        return started

    def finish(k, carry):
        pltpu.make_async_copy(tiles_ref.at[0], out_ref.at[0], sem).wait()
        return carry

    started = lax.fori_loop(0, slots // LOAD_UNROLL, start, 0)
    lax.fori_loop(0, started, finish, 0)


def pair_kernel(x_ref, other_ref, out_ref):
    first = lax.axis_index("core") == 0
    mine, other = x_ref[...], other_ref[...]
    feats = mine.shape[0]
    out_ref[:feats, :] = jnp.where(first, mine, other)
    out_ref[feats:, :] = jnp.where(first, other, mine)


def setup_kernel(
    live_ref, rows_in, cols_in, w1_in, w2_in, bias_in, x_in,
    place_ref, used_ref, weights_ref, x_ref, rows_ref, cols_ref, w1_ref, w2_ref, bias_ref, sems,
):
    sources = (rows_in, cols_in, w1_in, w2_in, bias_in, x_in)
    targets = (rows_ref, cols_ref, w1_ref, w2_ref, bias_ref, x_ref)
    copies = [
        pltpu.make_async_copy(source, target, sems.at[k])
        for k, (source, target) in enumerate(zip(sources, targets))
    ]
    for copy in copies:
        copy.start()
    for copy in copies:
        copy.wait()
    place_tiles(live_ref, rows_ref, cols_ref, place_ref, used_ref)
    pack_weights(w1_ref, w2_ref, bias_ref, weights_ref)


def place_tiles(live_ref, rows_ref, cols_ref, place_ref, used_ref):
    places = used_ref.shape[1]
    slots = rows_ref.shape[2]
    slot = lax.broadcasted_iota(jnp.int32, (1, slots), 1)
    rows = rows_ref[0]
    place = ((rows >> 2) * 2 + (rows & 1)) * (places // 16) + cols_ref[0]
    mine = (slot < live_ref[0, 0]) & (((rows >> 1) & 1) == lax.axis_index("core"))
    place = jnp.where(mine, place, -1)
    place_ref[...] = place
    here = lax.broadcasted_iota(jnp.int32, (places, slots), 0) == place
    onehot = jnp.where(here, 1.0, 0.0).astype(BF16)
    used = dot(jnp.ones((8, slots), BF16), onehot, ((1,), (1,)))
    used_ref[...] = used[0:1].astype(jnp.int32)


def bit_reversed(k):
    return (k & 1) << 2 | (k & 2) | k >> 2


def aggregate_kernel(used_ref, x0_ref, x1_ref, x2_ref, x3_ref, tiles_ref, out_ref, all_ref):
    feats, nodes = x0_ref.shape
    row, n_row = lax.axis_index("row"), lax.axis_size("row")
    for k, part in zip((0, *ORDER), (x0_ref, x1_ref, x2_ref, x3_ref)):
        source = row ^ k
        all_ref[:, pl.ds(pl.multiple_of(source * nodes, TILE), nodes)] = part[...]
    x_all = all_ref[...]
    groups = out_ref.shape[0]
    col_blocks = used_ref.shape[1] // (2 * groups)
    for group in range(groups):
        strips = []
        for block in (2 * group, 2 * group + 1):
            tiles = []
            for j in range(col_blocks):
                place = block * col_blocks + j
                tile = tiles_ref[place]
                tiles.append(jnp.where(used_ref[0, place] > 0, tile, jnp.zeros_like(tile)))
            strips.append(jnp.concatenate(tiles, 1))
        wide = dot(jnp.concatenate(strips, 0), x_all, ((1,), (1,))).T.astype(BF16)
        place = bit_reversed(group)
        out_ref[place, :feats, :] = wide[:, :TILE]
        out_ref[place, feats:, :] = wide[:, TILE:]


def pack_weights(w1_ref, w2_ref, bias_ref, out_ref):
    shape = (32, TILE)
    lane = lax.broadcasted_iota(jnp.int32, shape, 1)
    sub = lax.broadcasted_iota(jnp.int32, shape, 0)
    row = jnp.concatenate([bias_ref[...], jnp.zeros((1, TILE - 32), F32)], axis=1)
    bias = jnp.sum(jnp.where(lane == sub, row, 0.0), axis=1, keepdims=True)
    high = bias.astype(BF16).astype(F32)
    middle = (bias - high).astype(BF16).astype(F32)
    low = bias - high - middle
    rest = jnp.concatenate(
        [w2_ref[:, TILE:].astype(F32), jnp.zeros((32, TILE - REST), F32)], axis=1
    )
    for place, part in ((REST, high), (REST + 1, middle), (REST + 2, low)):
        rest = jnp.where(lane == place, part, rest)
    out_ref[:32, :] = w1_ref[...]
    out_ref[32:64, :] = w2_ref[:, :TILE]
    out_ref[64:, :] = rest.astype(BF16)

def total_kernel(parts_ref, weights_ref, out_ref):
    total = jnp.sum(parts_ref[...].astype(F32), axis=0).astype(BF16)
    rows = total.shape[0]
    out_ref[:rows, :] = total
    out_ref[rows:, :] = weights_ref[...]


def stack_kernel(*refs):
    for k, part in zip((0, *ORDER), refs[:-1]):
        refs[-1][k] = part[...]


def lanes16():
    return lax.broadcasted_iota(jnp.int32, (16, TILE), 1)

def is_fine(lane):
    return (lane == REST) | (lane == REST + 1) | (lane == HALF + REST)

def split_tail(tail):
    upper = tail.astype(BF16).astype(F32)
    moved = pltpu.roll(tail - upper, 2, 1)
    return jnp.where(is_fine(lanes16() - 2), moved, upper).astype(BF16)

def join_tail(tail):
    return jnp.where(is_fine(lanes16()), tail + pltpu.roll(tail, TILE - 2, 1), tail)

def node_kernel(mine_ref, other_ref, labels_ref, mask_ref, out_ref, y_ref):
    n_x = mine_ref.shape[0]
    x, core = lax.axis_index("x"), lax.axis_index("core")
    for ref, owner in ((mine_ref, core), (other_ref, 1 - core)):
        for k in range(n_x):
            feat = pl.multiple_of((x ^ k) * 32, 32)
            for b in range(2):
                node = pl.multiple_of((2 * owner + b) * TILE, TILE)
                y_ref[pl.ds(feat, 32), pl.ds(node, TILE)] = ref[k, 32 * b : 32 * b + 32, :]
    y = y_ref[...]

    def both(begin):
        rows = 32 * n_x
        return jnp.concatenate(
            [ref[:, begin : begin + 32, :].reshape(rows, TILE) for ref in (mine_ref, other_ref)], 0
        )

    w1, w2a, w2b = both(64), both(96), both(128)

    def bias_of(block):
        wide = block.astype(F32)
        return wide[:, REST : REST + 1] + wide[:, REST + 1 : REST + 2] + wide[:, REST + 2 : REST + 3]

    preact = dot(w1, y) + bias_of(w2b)
    _, t = gelu_parts(preact)
    hidden = (0.5 * preact * (1.0 + t)).astype(BF16)
    logits_a = dot(w2a, hidden, ((0,), (0,)))
    logits_b = dot(w2b, hidden, ((0,), (0,)))[:48]
    labels = labels_ref[...]
    mask = mask_ref[...].astype(F32)
    class_a = lax.broadcasted_iota(jnp.int32, logits_a.shape, 0)
    class_b = lax.broadcasted_iota(jnp.int32, logits_b.shape, 0) + TILE
    logits_b = jnp.where(class_b < CLASSES, logits_b, -jnp.inf)
    top = jnp.maximum(
        jnp.max(logits_a, axis=0, keepdims=True), jnp.max(logits_b, axis=0, keepdims=True)
    )
    shifted_a = logits_a - top
    shifted_b = logits_b - top
    exp_a = jnp.exp(shifted_a)
    exp_b = jnp.exp(shifted_b)
    expsum = jnp.sum(exp_a, axis=0, keepdims=True) + jnp.sum(exp_b, axis=0, keepdims=True)
    hit_a = class_a == labels
    hit_b = class_b == labels
    picked = jnp.sum(jnp.where(hit_a, shifted_a, 0.0), axis=0, keepdims=True) + jnp.sum(
        jnp.where(hit_b, shifted_b, 0.0), axis=0, keepdims=True
    )
    loss = jnp.sum((jnp.log(expsum) - picked) * mask)
    count = jnp.sum(mask)
    inverse = 1.0 / expsum
    grad_a = ((exp_a * inverse - hit_a.astype(F32)) * mask).astype(BF16)
    grad_b = ((exp_b * inverse - hit_b.astype(F32)) * mask).astype(BF16)

    own_w1 = mine_ref[0, 64:96, :]
    own_w2a = mine_ref[0, 96:128, :]
    own_w2b = mine_ref[0, 128:, :]
    own_pre = dot(own_w1, y) + bias_of(own_w2b)
    squared, own_t = gelu_parts(own_pre)
    own_hidden = (0.5 * own_pre * (1.0 + own_t)).astype(BF16)
    slope = 0.5 * (1.0 + own_t) + 0.5 * own_pre * (1.0 - own_t * own_t) * (
        GELU_SCALE * (1.0 + 3.0 * GELU_CUBE * squared)
    )
    grad_hidden = dot(own_w2a, grad_a) + dot(own_w2b[:, :48], grad_b)
    grad_pre = (grad_hidden * slope).astype(BF16)
    grad_b1 = jnp.sum(grad_pre.astype(F32), axis=1, keepdims=True)
    grad_w1 = dot(grad_pre, y, ((1,), (1,))).astype(BF16)
    grad_w2a = dot(own_hidden, grad_a, ((1,), (1,))).astype(BF16)
    grad_w2b = dot(own_hidden, grad_b, ((1,), (1,)))
    lane = lanes16()
    sub = lax.broadcasted_iota(jnp.int32, lane.shape, 0)
    wide = jnp.concatenate([grad_w2b, jnp.zeros((32, TILE - 48), F32)], axis=1)
    extra = jnp.where(sub == 0, loss, jnp.where(sub == 1, count, 0.0))
    tail = jnp.where(lane < HALF, wide[:16], pltpu.roll(wide[16:], HALF, 1))
    tail = jnp.where(lane == REST, grad_b1[:16], tail)
    tail = jnp.where(lane == REST + 1, extra, tail)
    tail = jnp.where(lane == HALF + REST, grad_b1[16:], tail)
    tail = split_tail(tail)
    out_ref[:32, :] = grad_w1
    out_ref[32:64, :] = grad_w2a
    out_ref[64:, :] = tail


def middle_kernel(*refs):
    out_ref = refs[-1]
    total = sum(part[...].astype(F32) for part in refs[:-1])
    tail = split_tail(join_tail(total[64:]))
    for k in range(out_ref.shape[0]):
        out_ref[k, :64, :] = total[:64].astype(BF16)
        out_ref[k, 64:, :] = tail

def final_kernel(parts_ref, w1_ref, w2_ref, b1_ref, loss_ref):
    total = jnp.sum(parts_ref[...].astype(F32), axis=0)
    tail = join_tail(total[64:])
    inverse = 1.0 / tail[1:2, REST + 1 : REST + 2]
    w1_ref[...] = total[:32] * inverse
    w2_ref[:, :TILE] = total[32:64] * inverse
    w2_ref[:16, TILE:] = tail[:, :REST] * inverse
    w2_ref[16:, TILE:] = pltpu.roll(tail, HALF, 1)[:, :REST] * inverse
    column = jnp.concatenate(
        [tail[:, REST : REST + 1], tail[:, HALF + REST : HALF + REST + 1]], axis=0
    )
    square = (32, 32)
    eye = lax.broadcasted_iota(jnp.int32, square, 0) == lax.broadcasted_iota(jnp.int32, square, 1)
    b1_ref[...] = jnp.sum(jnp.where(eye, column, 0.0), axis=0, keepdims=True) * inverse
    loss_ref[...] = tail[0:1, REST + 1 : REST + 2] * inverse

def exchanged(value, axis):
    size = lax.axis_size(axis)
    return [
        lax.ppermute(value, axis, [(k, k ^ step) for k in range(size)])
        for step in ORDER
    ]


def on_device(
    features,
    weight_in,
    bias,
    weight_out,
    adj_tiles,
    tile_rows,
    tile_cols,
    tile_live,
    labels,
    label_mask,
):
    n_row, n_col = lax.axis_size("row"), lax.axis_size(COL_BITS)
    n_core = lax.axis_size("core")
    n_feat = lax.axis_size("x") * n_core
    nodes, feats = features.shape
    row_blocks = nodes * n_col // TILE
    col_blocks = nodes * n_row // TILE
    grad_rows = 80

    x_mine = features.T
    x_other = lax.ppermute(x_mine, "core", [(0, 1), (1, 0)])
    tiles = pltpu.with_memory_space_constraint(
        adj_tiles.reshape(adj_tiles.shape[2:]), pltpu.HBM
    )
    places = row_blocks // 2 * col_blocks
    small = (tile_rows, tile_cols, weight_in.T, weight_out, bias.reshape(1, -1), x_mine)
    place, used, weights, x_mine = pl.pallas_call(
        setup_kernel,
        out_shape=(
            pltpu.VMEM((1, tiles.shape[0]), jnp.int32),
            pltpu.VMEM((1, places), jnp.int32),
            pltpu.VMEM((96, TILE), BF16),
            pltpu.VMEM(x_mine.shape, BF16),
        ),
        in_specs=[IN_SMEM] + [pl.BlockSpec(memory_space=pltpu.HBM)] * 6,
        out_specs=(IN_VMEM,) * 4,
        scratch_shapes=[pltpu.VMEM(v.shape, v.dtype) for v in small[:5]]
        + [pltpu.SemaphoreType.DMA((6,))],
        compiler_params=pltpu.CompilerParams(vmem_limit_bytes=8 * 2**20),
    )(tile_live, *(pltpu.with_memory_space_constraint(v, pltpu.HBM) for v in small))
    x_pair = call(pair_kernel, pltpu.VMEM((2 * feats, nodes), BF16), x_mine, x_other)
    x_rows = exchanged(x_pair, "row")
    loaded = pl.pallas_call(
        load_kernel,
        out_shape=pltpu.VMEM((places, TILE, TILE), BF16),
        in_specs=[IN_SMEM, pl.BlockSpec(memory_space=pltpu.HBM), IN_VMEM],
        out_specs=IN_VMEM,
        scratch_shapes=[pltpu.SemaphoreType.DMA],
        compiler_params=pltpu.CompilerParams(vmem_limit_bytes=2**20),
        cost_estimate=pl.CostEstimate(
            flops=0, bytes_accessed=2 * tiles.size, transcendentals=0
        ),
    )(place, tiles, pltpu.with_memory_space_constraint(x_pair, pltpu.VMEM))
    partial = call(
        aggregate_kernel,
        pltpu.VMEM((n_col, 4 * feats, TILE), BF16),
        used,
        x_pair,
        *x_rows,
        loaded,
        scalars=1,
        scratch=[pltpu.VMEM((2 * feats, n_row * nodes), BF16)],
    )
    parts = lax.all_to_all(partial, COL_BITS, 0, 0)
    rows = parts.shape[1] + weights.shape[0]
    message = call(total_kernel, pltpu.VMEM((rows, TILE), BF16), parts, weights)
    messages = (message, *exchanged(message, "x"))
    mine = call(stack_kernel, pltpu.VMEM((len(messages), rows, TILE), BF16), *messages)
    other = lax.ppermute(mine, "core", [(0, 1), (1, 0)])
    grads = call(
        node_kernel,
        pltpu.VMEM((grad_rows, TILE), BF16),
        mine,
        other,
        labels.reshape(1, -1),
        label_mask.reshape(1, -1),
        scratch=[pltpu.VMEM((feats * n_feat, nodes), BF16)],
    )
    grads = call(
        middle_kernel,
        pltpu.VMEM((n_col, grad_rows, TILE), BF16),
        grads,
        *exchanged(grads, "row"),
    )
    grads = lax.all_to_all(grads, COL_BITS, 0, 0)
    w1, w2, b1, loss = call(
        final_kernel,
        (
            jax.ShapeDtypeStruct((32, TILE), F32),
            jax.ShapeDtypeStruct((32, CLASSES), F32),
            jax.ShapeDtypeStruct((1, 32), F32),
            jax.ShapeDtypeStruct((1, 1), F32),
        ),
        grads,
    )
    return (loss.reshape(()), w1.T, b1.reshape(-1), w2)

def solution(mesh):
    shape = mesh.devices.shape
    split = jax.sharding.Mesh(
        mesh.devices.reshape(shape[0], 2, 2, 2, shape[2] // 2, 2),
        ("row", "c2", "c1", "c0", "x", "core"),
    )
    col, feat = ("c2", "c1", "c0"), ("x", "core")
    in_specs = (
        P((*col, "row"), feat),
        P(None, feat),
        P(feat),
        P(feat, None),
        P("row", col, None, None, None),
        P("row", col, None),
        P("row", col, None),
        P("row", col),
        P(("row", *col)),
        P(("row", *col)),
    )
    out_specs = (P(), P(None, feat), P(feat), P(feat, None))
    return jax.shard_map(
        on_device, mesh=split, in_specs=in_specs, out_specs=out_specs, check_vma=False
    )
```

```python
import functools

import jax
import jax.numpy as jnp
from jax import lax
from jax.experimental import pallas as pl
from jax.experimental.pallas import tpu as pltpu
from jax.sharding import PartitionSpec as P

CLASSES = 172
TILE = 128
REST = CLASSES - TILE
HALF = TILE // 2
GELU_SCALE = 0.7978845608028654
GELU_CUBE = 0.044715
LOAD_UNROLL = 16
COL_BITS = ("c0", "c1", "c2")
ORDER = (1, 3, 2)
F32 = jnp.float32
BF16 = jnp.bfloat16
IN_VMEM = pl.BlockSpec(memory_space=pltpu.VMEM)
IN_SMEM = pl.BlockSpec(memory_space=pltpu.SMEM)

def dot(a, b, contract=((1,), (0,))):
    return lax.dot_general(a, b, (contract, ((), ())), preferred_element_type=F32)

def gelu_parts(v):
    squared = v * v
    t = jnp.tanh(GELU_SCALE * v * (1.0 + GELU_CUBE * squared))
    return squared, t

def call(kernel, out_shape, *args, scalars=0, scratch=(), limit=16 * 2**20, cost=None):
    placed = args[:scalars] + tuple(
        pltpu.with_memory_space_constraint(arg, pltpu.VMEM) for arg in args[scalars:]
    )
    many = isinstance(out_shape, tuple)
    return pl.pallas_call(
        kernel,
        out_shape=out_shape,
        in_specs=[IN_SMEM] * scalars + [IN_VMEM] * (len(args) - scalars),
        out_specs=(IN_VMEM,) * len(out_shape) if many else IN_VMEM,
        scratch_shapes=scratch,
        compiler_params=pltpu.CompilerParams(vmem_limit_bytes=limit),
        cost_estimate=cost,
    )(*placed)

def load_kernel(live_ref, place_ref, tiles_ref, after_ref, out_ref, sem):
    del after_ref
    live = jnp.minimum(live_ref[0, 0], tiles_ref.shape[0])

    def start(trip, started):
        for part in range(LOAD_UNROLL):
            slot = trip * LOAD_UNROLL + part
            place = place_ref[0, slot]
            mine = (place >= 0) & (slot < live)

            @pl.when(mine)
            def _():
                pltpu.make_async_copy(tiles_ref.at[slot], out_ref.at[place], sem).start()

            started = started + mine.astype(jnp.int32)
        return started

    def finish(k, carry):
        pltpu.make_async_copy(tiles_ref.at[0], out_ref.at[0], sem).wait()
        return carry

    started = lax.fori_loop(0, (live + LOAD_UNROLL - 1) // LOAD_UNROLL, start, 0)
    lax.fori_loop(0, started, finish, 0)


def pair_kernel(x_ref, other_ref, out_ref):
    first = lax.axis_index("core") == 0
    mine, other = x_ref[...], other_ref[...]
    feats = mine.shape[0]
    out_ref[:feats, :] = jnp.where(first, mine, other)
    out_ref[feats:, :] = jnp.where(first, other, mine)


def setup_kernel(
    rows_in, cols_in, w1_in, w2_in, bias_in, x_in,
    place_ref, slot_ref, weights_ref, x_ref, rows_ref, cols_ref, w1_ref, w2_ref, bias_ref, place_vmem, slot_vmem, sems,
):
    sources = (rows_in, cols_in, w1_in, w2_in, bias_in, x_in)
    targets = (rows_ref, cols_ref, w1_ref, w2_ref, bias_ref, x_ref)
    copies = [
        pltpu.make_async_copy(source, target, sems.at[k])
        for k, (source, target) in enumerate(zip(sources, targets))
    ]
    for copy in copies:
        copy.start()
    for copy in copies:
        copy.wait()
    place_tiles(rows_ref, cols_ref, place_vmem, slot_vmem)
    maps = (
        pltpu.make_async_copy(place_vmem, place_ref, sems.at[0]),
        pltpu.make_async_copy(slot_vmem, slot_ref, sems.at[1]),
    )
    for copy in maps:
        copy.start()
    pack_weights(w1_ref, w2_ref, bias_ref, weights_ref)
    for copy in maps:
        copy.wait()


def place_tiles(rows_ref, cols_ref, place_ref, slot_ref):
    places = slot_ref.shape[1]
    slots = rows_ref.shape[2]
    rows = rows_ref[0]
    place = ((rows >> 2) * 2 + (rows & 1)) * (places // 16) + cols_ref[0]
    place = jnp.where(((rows >> 1) & 1) == lax.axis_index("core"), place, -1)
    place_ref[...] = place
    here = lax.broadcasted_iota(jnp.int32, (places, slots), 0) == place
    onehot = jnp.where(here, 1.0, 0.0).astype(BF16)
    number = lax.broadcasted_iota(jnp.int32, (8, slots), 1) + 1
    digit = lax.broadcasted_iota(jnp.int32, (8, slots), 0)
    digits = jnp.where(digit == 0, number & 127, jnp.where(digit == 1, number >> 7, 0))
    found = dot(digits.astype(F32).astype(BF16), onehot, ((1,), (1,)))
    slot_ref[...] = (found[0:1] + 128.0 * found[1:2]).astype(jnp.int32) - 1


def bit_reversed(k):
    return (k & 1) << 2 | (k & 2) | k >> 2


def aggregate_kernel(live_ref, slot_ref, x0_ref, x1_ref, x2_ref, x3_ref, tiles_ref, out_ref, all_ref):
    feats, nodes = x0_ref.shape
    row, n_row = lax.axis_index("row"), lax.axis_size("row")
    for k, part in zip((0, *ORDER), (x0_ref, x1_ref, x2_ref, x3_ref)):
        source = row ^ k
        all_ref[:, pl.ds(pl.multiple_of(source * nodes, TILE), nodes)] = part[...]
    x_all = all_ref[...]
    live = live_ref[0, 0]
    groups = out_ref.shape[0]
    col_blocks = slot_ref.shape[1] // (2 * groups)
    for group in range(groups):
        strips = []
        for block in (2 * group, 2 * group + 1):
            tiles = []
            for j in range(col_blocks):
                place = block * col_blocks + j
                tile = tiles_ref[place]
                slot = slot_ref[0, place]
                here = (slot >= 0) & (slot < live)
                tiles.append(jnp.where(here, tile, jnp.zeros_like(tile)))
            strips.append(jnp.concatenate(tiles, 1))
        wide = dot(jnp.concatenate(strips, 0), x_all, ((1,), (1,))).T.astype(BF16)
        place = bit_reversed(group)
        out_ref[place, :feats, :] = wide[:, :TILE]
        out_ref[place, feats:, :] = wide[:, TILE:]


def pack_weights(w1_ref, w2_ref, bias_ref, out_ref):
    shape = (32, TILE)
    lane = lax.broadcasted_iota(jnp.int32, shape, 1)
    sub = lax.broadcasted_iota(jnp.int32, shape, 0)
    row = jnp.concatenate([bias_ref[...], jnp.zeros((1, TILE - 32), F32)], axis=1)
    bias = jnp.sum(jnp.where(lane == sub, row, 0.0), axis=1, keepdims=True)
    high = bias.astype(BF16).astype(F32)
    middle = (bias - high).astype(BF16).astype(F32)
    low = bias - high - middle
    rest = jnp.concatenate(
        [w2_ref[:, TILE:].astype(F32), jnp.zeros((32, TILE - REST), F32)], axis=1
    )
    for place, part in ((REST, high), (REST + 1, middle), (REST + 2, low)):
        rest = jnp.where(lane == place, part, rest)
    out_ref[:32, :] = w1_ref[...]
    out_ref[32:64, :] = w2_ref[:, :TILE]
    out_ref[64:, :] = rest.astype(BF16)

def total_kernel(parts_ref, weights_ref, out_ref):
    total = jnp.sum(parts_ref[...].astype(F32), axis=0).astype(BF16)
    rows = total.shape[0]
    out_ref[:rows, :] = total
    out_ref[rows:, :] = weights_ref[...]


def stack_kernel(*refs):
    for k, part in zip((0, *ORDER), refs[:-1]):
        refs[-1][k] = part[...]


def lanes16():
    return lax.broadcasted_iota(jnp.int32, (16, TILE), 1)

def is_fine(lane):
    return (lane == REST) | (lane == REST + 1) | (lane == HALF + REST)

def split_tail(tail):
    upper = tail.astype(BF16).astype(F32)
    moved = pltpu.roll(tail - upper, 2, 1)
    return jnp.where(is_fine(lanes16() - 2), moved, upper).astype(BF16)

def join_tail(tail):
    return jnp.where(is_fine(lanes16()), tail + pltpu.roll(tail, TILE - 2, 1), tail)

def node_kernel(mine_ref, other_ref, labels_ref, mask_ref, out_ref, y_ref):
    n_x = mine_ref.shape[0]
    x, core = lax.axis_index("x"), lax.axis_index("core")
    for ref, owner in ((mine_ref, core), (other_ref, 1 - core)):
        for k in range(n_x):
            feat = pl.multiple_of((x ^ k) * 32, 32)
            for b in range(2):
                node = pl.multiple_of((2 * owner + b) * TILE, TILE)
                y_ref[pl.ds(feat, 32), pl.ds(node, TILE)] = ref[k, 32 * b : 32 * b + 32, :]
    y = y_ref[...]

    def both(begin):
        rows = 32 * n_x
        return jnp.concatenate(
            [ref[:, begin : begin + 32, :].reshape(rows, TILE) for ref in (mine_ref, other_ref)], 0
        )

    w1, w2a, w2b = both(64), both(96), both(128)

    def bias_of(block):
        wide = block.astype(F32)
        return wide[:, REST : REST + 1] + wide[:, REST + 1 : REST + 2] + wide[:, REST + 2 : REST + 3]

    preact = dot(w1, y) + bias_of(w2b)
    _, t = gelu_parts(preact)
    hidden = (0.5 * preact * (1.0 + t)).astype(BF16)
    logits_a = dot(w2a, hidden, ((0,), (0,)))
    logits_b = dot(w2b, hidden, ((0,), (0,)))[:48]
    labels = labels_ref[...]
    mask = mask_ref[...].astype(F32)
    class_a = lax.broadcasted_iota(jnp.int32, logits_a.shape, 0)
    class_b = lax.broadcasted_iota(jnp.int32, logits_b.shape, 0) + TILE
    logits_b = jnp.where(class_b < CLASSES, logits_b, -jnp.inf)
    top = jnp.maximum(
        jnp.max(logits_a, axis=0, keepdims=True), jnp.max(logits_b, axis=0, keepdims=True)
    )
    shifted_a = logits_a - top
    shifted_b = logits_b - top
    exp_a = jnp.exp(shifted_a)
    exp_b = jnp.exp(shifted_b)
    expsum = jnp.sum(exp_a, axis=0, keepdims=True) + jnp.sum(exp_b, axis=0, keepdims=True)
    hit_a = class_a == labels
    hit_b = class_b == labels
    picked = jnp.sum(jnp.where(hit_a, shifted_a, 0.0), axis=0, keepdims=True) + jnp.sum(
        jnp.where(hit_b, shifted_b, 0.0), axis=0, keepdims=True
    )
    loss = jnp.sum((jnp.log(expsum) - picked) * mask)
    count = jnp.sum(mask)
    inverse = 1.0 / expsum
    grad_a = ((exp_a * inverse - hit_a.astype(F32)) * mask).astype(BF16)
    grad_b = ((exp_b * inverse - hit_b.astype(F32)) * mask).astype(BF16)

    own_w1 = mine_ref[0, 64:96, :]
    own_w2a = mine_ref[0, 96:128, :]
    own_w2b = mine_ref[0, 128:, :]
    own_pre = dot(own_w1, y) + bias_of(own_w2b)
    squared, own_t = gelu_parts(own_pre)
    own_hidden = (0.5 * own_pre * (1.0 + own_t)).astype(BF16)
    slope = 0.5 * (1.0 + own_t) + 0.5 * own_pre * (1.0 - own_t * own_t) * (
        GELU_SCALE * (1.0 + 3.0 * GELU_CUBE * squared)
    )
    grad_hidden = dot(own_w2a, grad_a) + dot(own_w2b[:, :48], grad_b)
    grad_pre = (grad_hidden * slope).astype(BF16)
    grad_b1 = jnp.sum(grad_pre.astype(F32), axis=1, keepdims=True)
    grad_w1 = dot(grad_pre, y, ((1,), (1,))).astype(BF16)
    grad_w2a = dot(own_hidden, grad_a, ((1,), (1,))).astype(BF16)
    grad_w2b = dot(own_hidden, grad_b, ((1,), (1,)))
    lane = lanes16()
    sub = lax.broadcasted_iota(jnp.int32, lane.shape, 0)
    wide = jnp.concatenate([grad_w2b, jnp.zeros((32, TILE - 48), F32)], axis=1)
    extra = jnp.where(sub == 0, loss, jnp.where(sub == 1, count, 0.0))
    tail = jnp.where(lane < HALF, wide[:16], pltpu.roll(wide[16:], HALF, 1))
    tail = jnp.where(lane == REST, grad_b1[:16], tail)
    tail = jnp.where(lane == REST + 1, extra, tail)
    tail = jnp.where(lane == HALF + REST, grad_b1[16:], tail)
    tail = split_tail(tail)
    out_ref[:32, :] = grad_w1
    out_ref[32:64, :] = grad_w2a
    out_ref[64:, :] = tail


def middle_kernel(*refs):
    out_ref = refs[-1]
    total = sum(part[...].astype(F32) for part in refs[:-1])
    tail = split_tail(join_tail(total[64:]))
    for k in range(out_ref.shape[0]):
        out_ref[k, :64, :] = total[:64].astype(BF16)
        out_ref[k, 64:, :] = tail

def final_kernel(parts_ref, w1_ref, w2_ref, b1_ref, loss_ref):
    total = jnp.sum(parts_ref[...].astype(F32), axis=0)
    tail = join_tail(total[64:])
    inverse = 1.0 / tail[1:2, REST + 1 : REST + 2]
    w1_ref[...] = total[:32] * inverse
    w2_ref[:, :TILE] = total[32:64] * inverse
    w2_ref[:16, TILE:] = tail[:, :REST] * inverse
    w2_ref[16:, TILE:] = pltpu.roll(tail, HALF, 1)[:, :REST] * inverse
    column = jnp.concatenate(
        [tail[:, REST : REST + 1], tail[:, HALF + REST : HALF + REST + 1]], axis=0
    )
    square = (32, 32)
    eye = lax.broadcasted_iota(jnp.int32, square, 0) == lax.broadcasted_iota(jnp.int32, square, 1)
    b1_ref[...] = jnp.sum(jnp.where(eye, column, 0.0), axis=0, keepdims=True) * inverse
    loss_ref[...] = tail[0:1, REST + 1 : REST + 2] * inverse

def exchanged(value, axis):
    size = lax.axis_size(axis)
    return [
        lax.ppermute(value, axis, [(k, k ^ step) for k in range(size)])
        for step in ORDER
    ]


def on_device(
    features,
    weight_in,
    bias,
    weight_out,
    adj_tiles,
    tile_rows,
    tile_cols,
    tile_live,
    labels,
    label_mask,
):
    n_row, n_col = lax.axis_size("row"), lax.axis_size(COL_BITS)
    n_core = lax.axis_size("core")
    n_feat = lax.axis_size("x") * n_core
    nodes, feats = features.shape
    row_blocks = nodes * n_col // TILE
    col_blocks = nodes * n_row // TILE
    grad_rows = 80

    x_mine = features.T
    x_other = lax.ppermute(x_mine, "core", [(0, 1), (1, 0)])
    tiles = pltpu.with_memory_space_constraint(
        adj_tiles.reshape(adj_tiles.shape[2:]), pltpu.HBM
    )
    places = row_blocks // 2 * col_blocks
    small = (tile_rows, tile_cols, weight_in.T, weight_out, bias.reshape(1, -1), x_mine)
    place, slots, weights, x_mine = pl.pallas_call(
        setup_kernel,
        out_shape=(
            pltpu.SMEM((1, tiles.shape[0]), jnp.int32),
            pltpu.SMEM((1, places), jnp.int32),
            pltpu.VMEM((96, TILE), BF16),
            pltpu.VMEM(x_mine.shape, BF16),
        ),
        in_specs=[pl.BlockSpec(memory_space=pltpu.HBM)] * 6,
        out_specs=(IN_SMEM, IN_SMEM, IN_VMEM, IN_VMEM),
        scratch_shapes=[pltpu.VMEM(v.shape, v.dtype) for v in small[:5]]
        + [pltpu.VMEM((1, tiles.shape[0]), jnp.int32), pltpu.VMEM((1, places), jnp.int32)]
        + [pltpu.SemaphoreType.DMA((6,))],
        compiler_params=pltpu.CompilerParams(vmem_limit_bytes=8 * 2**20),
    )(*(pltpu.with_memory_space_constraint(v, pltpu.HBM) for v in small))
    x_pair = call(pair_kernel, pltpu.VMEM((2 * feats, nodes), BF16), x_mine, x_other)
    x_rows = exchanged(x_pair, "row")
    loaded = pl.pallas_call(
        load_kernel,
        out_shape=pltpu.VMEM((places, TILE, TILE), BF16),
        in_specs=[IN_SMEM, IN_SMEM, pl.BlockSpec(memory_space=pltpu.HBM), IN_VMEM],
        out_specs=IN_VMEM,
        scratch_shapes=[pltpu.SemaphoreType.DMA],
        compiler_params=pltpu.CompilerParams(vmem_limit_bytes=2**20),
        cost_estimate=pl.CostEstimate(
            flops=0, bytes_accessed=2 * tiles.size, transcendentals=0
        ),
    )(tile_live, place, tiles, pltpu.with_memory_space_constraint(x_pair, pltpu.VMEM))
    partial = call(
        aggregate_kernel,
        pltpu.VMEM((n_col, 4 * feats, TILE), BF16),
        tile_live,
        slots,
        x_pair,
        *x_rows,
        loaded,
        scalars=2,
        scratch=[pltpu.VMEM((2 * feats, n_row * nodes), BF16)],
    )
    parts = lax.all_to_all(partial, COL_BITS, 0, 0)
    rows = parts.shape[1] + weights.shape[0]
    message = call(total_kernel, pltpu.VMEM((rows, TILE), BF16), parts, weights)
    messages = (message, *exchanged(message, "x"))
    mine = call(stack_kernel, pltpu.VMEM((len(messages), rows, TILE), BF16), *messages)
    other = lax.ppermute(mine, "core", [(0, 1), (1, 0)])
    grads = call(
        node_kernel,
        pltpu.VMEM((grad_rows, TILE), BF16),
        mine,
        other,
        labels.reshape(1, -1),
        label_mask.reshape(1, -1),
        scratch=[pltpu.VMEM((feats * n_feat, nodes), BF16)],
    )
    grads = call(
        middle_kernel,
        pltpu.VMEM((n_col, grad_rows, TILE), BF16),
        grads,
        *exchanged(grads, "row"),
    )
    grads = lax.all_to_all(grads, COL_BITS, 0, 0)
    w1, w2, b1, loss = call(
        final_kernel,
        (
            jax.ShapeDtypeStruct((32, TILE), F32),
            jax.ShapeDtypeStruct((32, CLASSES), F32),
            jax.ShapeDtypeStruct((1, 32), F32),
            jax.ShapeDtypeStruct((1, 1), F32),
        ),
        grads,
    )
    return (loss.reshape(()), w1.T, b1.reshape(-1), w2)

def solution(mesh):
    shape = mesh.devices.shape
    split = jax.sharding.Mesh(
        mesh.devices.reshape(shape[0], 2, 2, 2, shape[2] // 2, 2),
        ("row", "c2", "c1", "c0", "x", "core"),
    )
    col, feat = ("c2", "c1", "c0"), ("x", "core")
    in_specs = (
        P((*col, "row"), feat),
        P(None, feat),
        P(feat),
        P(feat, None),
        P("row", col, None, None, None),
        P("row", col, None),
        P("row", col, None),
        P("row", col),
        P(("row", *col)),
        P(("row", *col)),
    )
    out_specs = (P(), P(None, feat), P(feat), P(feat, None))
    return jax.shard_map(
        on_device, mesh=split, in_specs=in_specs, out_specs=out_specs, check_vma=False
    )
```

```python
import functools

import jax
import jax.numpy as jnp
from jax import lax
from jax.experimental import pallas as pl
from jax.experimental.pallas import tpu as pltpu
from jax.sharding import PartitionSpec as P

CLASSES = 172
TILE = 128
REST = CLASSES - TILE
HALF = TILE // 2
GELU_SCALE = 0.7978845608028654
GELU_CUBE = 0.044715
LOAD_UNROLL = 16
COL_BITS = ("c0", "c1", "c2")
ORDER = (1, 3, 2)
F32 = jnp.float32
BF16 = jnp.bfloat16
IN_VMEM = pl.BlockSpec(memory_space=pltpu.VMEM)
IN_SMEM = pl.BlockSpec(memory_space=pltpu.SMEM)

def dot(a, b, contract=((1,), (0,))):
    return lax.dot_general(a, b, (contract, ((), ())), preferred_element_type=F32)

def gelu_parts(v):
    squared = v * v
    t = jnp.tanh(GELU_SCALE * v * (1.0 + GELU_CUBE * squared))
    return squared, t

def call(kernel, out_shape, *args, scalars=0, scratch=(), limit=16 * 2**20, cost=None):
    placed = args[:scalars] + tuple(
        pltpu.with_memory_space_constraint(arg, pltpu.VMEM) for arg in args[scalars:]
    )
    many = isinstance(out_shape, tuple)
    return pl.pallas_call(
        kernel,
        out_shape=out_shape,
        in_specs=[IN_SMEM] * scalars + [IN_VMEM] * (len(args) - scalars),
        out_specs=(IN_VMEM,) * len(out_shape) if many else IN_VMEM,
        scratch_shapes=scratch,
        compiler_params=pltpu.CompilerParams(vmem_limit_bytes=limit),
        cost_estimate=cost,
    )(*placed)

def load_kernel(live_ref, place_ref, tiles_ref, after_ref, out_ref, sem):
    del after_ref
    live = jnp.minimum(live_ref[0, 0], tiles_ref.shape[0])

    def start(trip, started):
        for part in range(LOAD_UNROLL):
            slot = trip * LOAD_UNROLL + part
            place = place_ref[0, slot]
            mine = (place >= 0) & (slot < live)

            @pl.when(mine)
            def _():
                pltpu.make_async_copy(tiles_ref.at[slot], out_ref.at[place], sem).start()

            started = started + mine.astype(jnp.int32)
        return started

    def finish(k, carry):
        pltpu.make_async_copy(tiles_ref.at[0], out_ref.at[0], sem).wait()
        return carry

    started = lax.fori_loop(0, (live + LOAD_UNROLL - 1) // LOAD_UNROLL, start, 0)
    lax.fori_loop(0, started, finish, 0)


def pair_kernel(x_ref, other_ref, out_ref):
    first = lax.axis_index("core") == 0
    mine, other = x_ref[...], other_ref[...]
    feats = mine.shape[0]
    out_ref[:feats, :] = jnp.where(first, mine, other)
    out_ref[feats:, :] = jnp.where(first, other, mine)


def setup_kernel(
    rows_in, cols_in, w1_in, w2_in, bias_in, x_in,
    place_ref, slot_ref, weights_ref, x_ref, rows_ref, cols_ref, w1_ref, w2_ref, bias_ref, place_vmem, slot_vmem, sems,
):
    sources = (rows_in, cols_in, w1_in, w2_in, bias_in, x_in)
    targets = (rows_ref, cols_ref, w1_ref, w2_ref, bias_ref, x_ref)
    copies = [
        pltpu.make_async_copy(source, target, sems.at[k])
        for k, (source, target) in enumerate(zip(sources, targets))
    ]
    for copy in copies:
        copy.start()
    for copy in copies[:2]:
        copy.wait()
    maps = (
        pltpu.make_async_copy(place_vmem, place_ref, sems.at[6]),
        pltpu.make_async_copy(slot_vmem, slot_ref, sems.at[7]),
    )
    place = places_of(rows_ref, cols_ref, slot_ref.shape[1])
    place_vmem[...] = place
    maps[0].start()
    slot_vmem[...] = slots_of(place, slot_ref.shape[1])
    maps[1].start()
    for copy in copies[2:]:
        copy.wait()
    pack_weights(w1_ref, w2_ref, bias_ref, weights_ref)
    for copy in maps:
        copy.wait()


def places_of(rows_ref, cols_ref, places):
    rows = rows_ref[0]
    place = ((rows >> 2) * 2 + (rows & 1)) * (places // 16) + cols_ref[0]
    return jnp.where(((rows >> 1) & 1) == lax.axis_index("core"), place, -1)


def slots_of(place, places):
    slots = place.shape[1]
    here = lax.broadcasted_iota(jnp.int32, (places, slots), 0) == place
    onehot = jnp.where(here, 1.0, 0.0).astype(BF16)
    number = lax.broadcasted_iota(jnp.int32, (8, slots), 1) + 1
    digit = lax.broadcasted_iota(jnp.int32, (8, slots), 0)
    digits = jnp.where(digit == 0, number & 127, jnp.where(digit == 1, number >> 7, 0))
    found = dot(digits.astype(F32).astype(BF16), onehot, ((1,), (1,)))
    return (found[0:1] + 128.0 * found[1:2]).astype(jnp.int32) - 1


def bit_reversed(k):
    return (k & 1) << 2 | (k & 2) | k >> 2


def aggregate_kernel(live_ref, slot_ref, x0_ref, x1_ref, x2_ref, x3_ref, tiles_ref, out_ref, all_ref):
    feats, nodes = x0_ref.shape
    row, n_row = lax.axis_index("row"), lax.axis_size("row")
    for k, part in zip((0, *ORDER), (x0_ref, x1_ref, x2_ref, x3_ref)):
        source = row ^ k
        all_ref[:, pl.ds(pl.multiple_of(source * nodes, TILE), nodes)] = part[...]
    x_all = all_ref[...]
    live = live_ref[0, 0]
    groups = out_ref.shape[0]
    col_blocks = slot_ref.shape[1] // (2 * groups)
    for group in range(groups):
        strips = []
        for block in (2 * group, 2 * group + 1):
            tiles = []
            for j in range(col_blocks):
                place = block * col_blocks + j
                tile = tiles_ref[place]
                slot = slot_ref[0, place]
                here = (slot >= 0) & (slot < live)
                tiles.append(jnp.where(here, tile, jnp.zeros_like(tile)))
            strips.append(jnp.concatenate(tiles, 1))
        wide = dot(jnp.concatenate(strips, 0), x_all, ((1,), (1,))).T.astype(BF16)
        place = bit_reversed(group)
        out_ref[place, :feats, :] = wide[:, :TILE]
        out_ref[place, feats:, :] = wide[:, TILE:]


def pack_weights(w1_ref, w2_ref, bias_ref, out_ref):
    shape = (32, TILE)
    lane = lax.broadcasted_iota(jnp.int32, shape, 1)
    sub = lax.broadcasted_iota(jnp.int32, shape, 0)
    row = jnp.concatenate([bias_ref[...], jnp.zeros((1, TILE - 32), F32)], axis=1)
    bias = jnp.sum(jnp.where(lane == sub, row, 0.0), axis=1, keepdims=True)
    high = bias.astype(BF16).astype(F32)
    middle = (bias - high).astype(BF16).astype(F32)
    low = bias - high - middle
    rest = jnp.concatenate(
        [w2_ref[:, TILE:].astype(F32), jnp.zeros((32, TILE - REST), F32)], axis=1
    )
    for place, part in ((REST, high), (REST + 1, middle), (REST + 2, low)):
        rest = jnp.where(lane == place, part, rest)
    out_ref[:32, :] = w1_ref[...]
    out_ref[32:64, :] = w2_ref[:, :TILE]
    out_ref[64:, :] = rest.astype(BF16)

def total_kernel(parts_ref, weights_ref, out_ref):
    total = jnp.sum(parts_ref[...].astype(F32), axis=0).astype(BF16)
    rows = total.shape[0]
    out_ref[:rows, :] = total
    out_ref[rows:, :] = weights_ref[...]


def stack_kernel(*refs):
    for k, part in zip((0, *ORDER), refs[:-1]):
        refs[-1][k] = part[...]


def lanes16():
    return lax.broadcasted_iota(jnp.int32, (16, TILE), 1)

def is_fine(lane):
    return (lane == REST) | (lane == REST + 1) | (lane == HALF + REST)

def split_tail(tail):
    upper = tail.astype(BF16).astype(F32)
    moved = pltpu.roll(tail - upper, 2, 1)
    return jnp.where(is_fine(lanes16() - 2), moved, upper).astype(BF16)

def join_tail(tail):
    return jnp.where(is_fine(lanes16()), tail + pltpu.roll(tail, TILE - 2, 1), tail)

def node_kernel(mine_ref, other_ref, labels_ref, mask_ref, out_ref, y_ref):
    n_x = mine_ref.shape[0]
    x, core = lax.axis_index("x"), lax.axis_index("core")
    for ref, owner in ((mine_ref, core), (other_ref, 1 - core)):
        for k in range(n_x):
            feat = pl.multiple_of((x ^ k) * 32, 32)
            for b in range(2):
                node = pl.multiple_of((2 * owner + b) * TILE, TILE)
                y_ref[pl.ds(feat, 32), pl.ds(node, TILE)] = ref[k, 32 * b : 32 * b + 32, :]
    y = y_ref[...]

    def both(begin):
        rows = 32 * n_x
        return jnp.concatenate(
            [ref[:, begin : begin + 32, :].reshape(rows, TILE) for ref in (mine_ref, other_ref)], 0
        )

    w1, w2a, w2b = both(64), both(96), both(128)

    def bias_of(block):
        wide = block.astype(F32)
        return wide[:, REST : REST + 1] + wide[:, REST + 1 : REST + 2] + wide[:, REST + 2 : REST + 3]

    preact = dot(w1, y) + bias_of(w2b)
    _, t = gelu_parts(preact)
    hidden = (0.5 * preact * (1.0 + t)).astype(BF16)
    logits_a = dot(w2a, hidden, ((0,), (0,)))
    logits_b = dot(w2b, hidden, ((0,), (0,)))[:48]
    labels = labels_ref[...]
    mask = mask_ref[...].astype(F32)
    class_a = lax.broadcasted_iota(jnp.int32, logits_a.shape, 0)
    class_b = lax.broadcasted_iota(jnp.int32, logits_b.shape, 0) + TILE
    logits_b = jnp.where(class_b < CLASSES, logits_b, -jnp.inf)
    top = jnp.maximum(
        jnp.max(logits_a, axis=0, keepdims=True), jnp.max(logits_b, axis=0, keepdims=True)
    )
    shifted_a = logits_a - top
    shifted_b = logits_b - top
    exp_a = jnp.exp(shifted_a)
    exp_b = jnp.exp(shifted_b)
    expsum = jnp.sum(exp_a, axis=0, keepdims=True) + jnp.sum(exp_b, axis=0, keepdims=True)
    hit_a = class_a == labels
    hit_b = class_b == labels
    picked = jnp.sum(jnp.where(hit_a, shifted_a, 0.0), axis=0, keepdims=True) + jnp.sum(
        jnp.where(hit_b, shifted_b, 0.0), axis=0, keepdims=True
    )
    loss = jnp.sum((jnp.log(expsum) - picked) * mask)
    count = jnp.sum(mask)
    inverse = 1.0 / expsum
    grad_a = ((exp_a * inverse - hit_a.astype(F32)) * mask).astype(BF16)
    grad_b = ((exp_b * inverse - hit_b.astype(F32)) * mask).astype(BF16)

    own_w1 = mine_ref[0, 64:96, :]
    own_w2a = mine_ref[0, 96:128, :]
    own_w2b = mine_ref[0, 128:, :]
    own_pre = dot(own_w1, y) + bias_of(own_w2b)
    squared, own_t = gelu_parts(own_pre)
    own_hidden = (0.5 * own_pre * (1.0 + own_t)).astype(BF16)
    slope = 0.5 * (1.0 + own_t) + 0.5 * own_pre * (1.0 - own_t * own_t) * (
        GELU_SCALE * (1.0 + 3.0 * GELU_CUBE * squared)
    )
    grad_hidden = dot(own_w2a, grad_a) + dot(own_w2b[:, :48], grad_b)
    grad_pre = (grad_hidden * slope).astype(BF16)
    grad_b1 = jnp.sum(grad_pre.astype(F32), axis=1, keepdims=True)
    grad_w1 = dot(grad_pre, y, ((1,), (1,))).astype(BF16)
    grad_w2a = dot(own_hidden, grad_a, ((1,), (1,))).astype(BF16)
    grad_w2b = dot(own_hidden, grad_b, ((1,), (1,)))
    lane = lanes16()
    sub = lax.broadcasted_iota(jnp.int32, lane.shape, 0)
    wide = jnp.concatenate([grad_w2b, jnp.zeros((32, TILE - 48), F32)], axis=1)
    extra = jnp.where(sub == 0, loss, jnp.where(sub == 1, count, 0.0))
    tail = jnp.where(lane < HALF, wide[:16], pltpu.roll(wide[16:], HALF, 1))
    tail = jnp.where(lane == REST, grad_b1[:16], tail)
    tail = jnp.where(lane == REST + 1, extra, tail)
    tail = jnp.where(lane == HALF + REST, grad_b1[16:], tail)
    tail = split_tail(tail)
    out_ref[:32, :] = grad_w1
    out_ref[32:64, :] = grad_w2a
    out_ref[64:, :] = tail


def middle_kernel(*refs):
    out_ref = refs[-1]
    total = sum(part[...].astype(F32) for part in refs[:-1])
    tail = split_tail(join_tail(total[64:]))
    for k in range(out_ref.shape[0]):
        out_ref[k, :64, :] = total[:64].astype(BF16)
        out_ref[k, 64:, :] = tail

def final_kernel(parts_ref, w1_ref, w2_ref, b1_ref, loss_ref):
    total = jnp.sum(parts_ref[...].astype(F32), axis=0)
    tail = join_tail(total[64:])
    inverse = 1.0 / tail[1:2, REST + 1 : REST + 2]
    w1_ref[...] = total[:32] * inverse
    w2_ref[:, :TILE] = total[32:64] * inverse
    w2_ref[:16, TILE:] = tail[:, :REST] * inverse
    w2_ref[16:, TILE:] = pltpu.roll(tail, HALF, 1)[:, :REST] * inverse
    column = jnp.concatenate(
        [tail[:, REST : REST + 1], tail[:, HALF + REST : HALF + REST + 1]], axis=0
    )
    square = (32, 32)
    eye = lax.broadcasted_iota(jnp.int32, square, 0) == lax.broadcasted_iota(jnp.int32, square, 1)
    b1_ref[...] = jnp.sum(jnp.where(eye, column, 0.0), axis=0, keepdims=True) * inverse
    loss_ref[...] = tail[0:1, REST + 1 : REST + 2] * inverse

def exchanged(value, axis):
    size = lax.axis_size(axis)
    return [
        lax.ppermute(value, axis, [(k, k ^ step) for k in range(size)])
        for step in ORDER
    ]


def on_device(
    features,
    weight_in,
    bias,
    weight_out,
    adj_tiles,
    tile_rows,
    tile_cols,
    tile_live,
    labels,
    label_mask,
):
    n_row, n_col = lax.axis_size("row"), lax.axis_size(COL_BITS)
    n_core = lax.axis_size("core")
    n_feat = lax.axis_size("x") * n_core
    nodes, feats = features.shape
    row_blocks = nodes * n_col // TILE
    col_blocks = nodes * n_row // TILE
    grad_rows = 80

    x_mine = features.T
    x_other = lax.ppermute(x_mine, "core", [(0, 1), (1, 0)])
    tiles = pltpu.with_memory_space_constraint(
        adj_tiles.reshape(adj_tiles.shape[2:]), pltpu.HBM
    )
    places = row_blocks // 2 * col_blocks
    small = (tile_rows, tile_cols, weight_in.T, weight_out, bias.reshape(1, -1), x_mine)
    place, slots, weights, x_mine = pl.pallas_call(
        setup_kernel,
        out_shape=(
            pltpu.SMEM((1, tiles.shape[0]), jnp.int32),
            pltpu.SMEM((1, places), jnp.int32),
            pltpu.VMEM((96, TILE), BF16),
            pltpu.VMEM(x_mine.shape, BF16),
        ),
        in_specs=[pl.BlockSpec(memory_space=pltpu.HBM)] * 6,
        out_specs=(IN_SMEM, IN_SMEM, IN_VMEM, IN_VMEM),
        scratch_shapes=[pltpu.VMEM(v.shape, v.dtype) for v in small[:5]]
        + [pltpu.VMEM((1, tiles.shape[0]), jnp.int32), pltpu.VMEM((1, places), jnp.int32)]
        + [pltpu.SemaphoreType.DMA((8,))],
        compiler_params=pltpu.CompilerParams(vmem_limit_bytes=8 * 2**20),
    )(*(pltpu.with_memory_space_constraint(v, pltpu.HBM) for v in small))
    x_pair = call(pair_kernel, pltpu.VMEM((2 * feats, nodes), BF16), x_mine, x_other)
    x_rows = exchanged(x_pair, "row")
    loaded = pl.pallas_call(
        load_kernel,
        out_shape=pltpu.VMEM((places, TILE, TILE), BF16),
        in_specs=[IN_SMEM, IN_SMEM, pl.BlockSpec(memory_space=pltpu.HBM), IN_VMEM],
        out_specs=IN_VMEM,
        scratch_shapes=[pltpu.SemaphoreType.DMA],
        compiler_params=pltpu.CompilerParams(vmem_limit_bytes=2**20),
        cost_estimate=pl.CostEstimate(
            flops=0, bytes_accessed=2 * tiles.size, transcendentals=0
        ),
    )(tile_live, place, tiles, pltpu.with_memory_space_constraint(x_pair, pltpu.VMEM))
    partial = call(
        aggregate_kernel,
        pltpu.VMEM((n_col, 4 * feats, TILE), BF16),
        tile_live,
        slots,
        x_pair,
        *x_rows,
        loaded,
        scalars=2,
        scratch=[pltpu.VMEM((2 * feats, n_row * nodes), BF16)],
    )
    parts = lax.all_to_all(partial, COL_BITS, 0, 0)
    rows = parts.shape[1] + weights.shape[0]
    message = call(total_kernel, pltpu.VMEM((rows, TILE), BF16), parts, weights)
    messages = (message, *exchanged(message, "x"))
    mine = call(stack_kernel, pltpu.VMEM((len(messages), rows, TILE), BF16), *messages)
    other = lax.ppermute(mine, "core", [(0, 1), (1, 0)])
    grads = call(
        node_kernel,
        pltpu.VMEM((grad_rows, TILE), BF16),
        mine,
        other,
        labels.reshape(1, -1),
        label_mask.reshape(1, -1),
        scratch=[pltpu.VMEM((feats * n_feat, nodes), BF16)],
    )
    grads = call(
        middle_kernel,
        pltpu.VMEM((n_col, grad_rows, TILE), BF16),
        grads,
        *exchanged(grads, "row"),
    )
    grads = lax.all_to_all(grads, COL_BITS, 0, 0)
    w1, w2, b1, loss = call(
        final_kernel,
        (
            jax.ShapeDtypeStruct((32, TILE), F32),
            jax.ShapeDtypeStruct((32, CLASSES), F32),
            jax.ShapeDtypeStruct((1, 32), F32),
            jax.ShapeDtypeStruct((1, 1), F32),
        ),
        grads,
    )
    return (loss.reshape(()), w1.T, b1.reshape(-1), w2)

def solution(mesh):
    shape = mesh.devices.shape
    split = jax.sharding.Mesh(
        mesh.devices.reshape(shape[0], 2, 2, 2, shape[2] // 2, 2),
        ("row", "c2", "c1", "c0", "x", "core"),
    )
    col, feat = ("c2", "c1", "c0"), ("x", "core")
    in_specs = (
        P((*col, "row"), feat),
        P(None, feat),
        P(feat),
        P(feat, None),
        P("row", col, None, None, None),
        P("row", col, None),
        P("row", col, None),
        P("row", col),
        P(("row", *col)),
        P(("row", *col)),
    )
    out_specs = (P(), P(None, feat), P(feat), P(feat, None))
    return jax.shard_map(
        on_device, mesh=split, in_specs=in_specs, out_specs=out_specs, check_vma=False
    )
```
